32 devices in a mesh: seq: 16 (over z, y, core), fsdp: 2 (over x).
Axes of the slice: x: 2, y: 2, z: 4, core: 2. Of those that a mesh axis runs over, the one named last changes fastest.
Arguments:
- tokens: float32 [1, 6144, 3072], P(None, 'seq', 'fsdp'), may hold values from -6 to 6
- block_mask: int32 [8, 6, 6], replicated, may hold values from 0 to 1, as said below
- space_qkv: bfloat16 [3072, 3, 512], P(None, None, 'fsdp'), may hold values from -0.109375 to 0.109375
- space_out: bfloat16 [512, 3072], P('fsdp'), may hold values from -0.375 to 0.375
- space_mod: float32 [3, 3072], replicated, may hold values from -2 to 3
- time_qkv: bfloat16 [3072, 3, 512], P(None, None, 'fsdp'), may hold values from -0.109375 to 0.109375
- time_out: bfloat16 [512, 3072], P('fsdp'), may hold values from -0.375 to 0.375
- time_mod: float32 [3, 3072], replicated, may hold values from -2 to 3
Outputs:
- result: float32 [1, 6144, 3072], P(None, 'seq', 'fsdp')
The draws below stay inside these ranges and needn't reach their ends.
Inputs may be any that keep to these rules, and one draw needn't show every extreme that they name: block_mask[f, i, i] = 1 for every frame f and block i.
All inputs are finite; a program needn't handle non-finite values.
Results may differ from the reference program's by a relative error of at most 0.015.
Values may be sent and summed in bfloat16 or wider, within the bound.
A program may use at most 128 MiB of HBM per device.

```python
import math
import jax
import jax.numpy as jnp
from jax import lax

D = 3072
HD = 128
P_SIZE = 768
BLOCK = 128
VIDEOS = 1
HEADS = 4
F = 8
TOKV = 6144
NB = 6
N_FSDP = 2


def draw_tokens(key, part):
    jitter = jax.random.normal(jax.random.fold_in(key, 11), (VIDEOS, TOKV, D), jnp.float32)
    values = jitter
    return jnp.clip(values, -6.0, 6.0).astype(jnp.float32)


def draw_block_mask(key, part):
    radius = jax.random.randint(jax.random.fold_in(key, 21), (F, NB, 1), 0, NB)
    row_ids = lax.broadcasted_iota(jnp.int32, (F, NB, NB), 1)
    col_ids = lax.broadcasted_iota(jnp.int32, (F, NB, NB), 2)
    return (jnp.abs(row_ids - col_ids) <= radius).astype(jnp.int32)


def draw_modulation(key, salt):
    folded = jax.random.fold_in(key, salt)
    shift_row = jnp.clip(0.5 * jax.random.normal(jax.random.fold_in(folded, 1), (D,), jnp.float32), -2.0, 2.0)
    scale_row = jnp.clip(0.3 * jax.random.normal(jax.random.fold_in(folded, 2), (D,), jnp.float32), -1.0, 1.0)
    gate_row = jax.random.uniform(jax.random.fold_in(folded, 3), (D,), jnp.float32, 0.3, 1.0)
    return jnp.stack([shift_row, scale_row, gate_row]).astype(jnp.float32)


def draw_space_mod(key, part):
    return draw_modulation(key, 31)


def draw_time_mod(key, part):
    return draw_modulation(key, 32)


def raised(entries, own_key, source, target, blocks, factor):
    owner, partner = [(jnp.arange(entries.shape[dim]) // (entries.shape[dim] // blocks)).reshape([-1 if axis == dim else 1 for axis in range(entries.ndim)]) for dim in (source, target)]
    chosen = jax.random.permutation(own_key, blocks)[partner]
    strong = (owner == chosen) | (owner == (partner + blocks // 2) % blocks)
    return jnp.where(strong, factor * entries, entries)


def block_levels(stream_key, dims, cuts, smallest, top_value):
    loudness = 1.0
    for position, parts in cuts:
        steps = jax.random.uniform(jax.random.fold_in(jax.random.fold_in(stream_key, 6), position), (parts,), jnp.float32, smallest / len(cuts), top_value / len(cuts))
        loudness = loudness * jnp.repeat(jnp.exp(steps), dims[position] // parts).reshape((-1,) + (1,) * (len(dims) - 1 - position))
    return loudness


def scatter_about(own_key, dims, deviation, reach, shards=(), dtype=jnp.bfloat16):
    drawn = deviation * jax.random.normal(own_key, dims, jnp.float32)
    if shards:
        drawn = drawn * block_levels(own_key, dims, shards, -0.22, 0.18)
    return jnp.clip(drawn, -reach, reach).astype(dtype)


def heavy_noise(own_key, extent, scale, limit, cuts, heavy, dtype=jnp.bfloat16):
    entries = scale * jax.random.normal(own_key, extent, jnp.float32)
    if cuts:
        entries = entries * block_levels(own_key, extent, cuts, -0.22, 0.18)
    return jnp.clip(raised(entries, jax.random.fold_in(own_key, 3), *heavy), -limit, limit).astype(dtype)


def setup_inputs(seed: int = 0) -> dict:
    arg_keys = jax.random.split(jax.random.key(seed), 9)
    tokens = draw_tokens(jax.random.fold_in(arg_keys[8], 71), 0)
    block_mask = draw_block_mask(jax.random.fold_in(arg_keys[8], 71), 0)
    space_qkv = scatter_about(arg_keys[2], (D, 3, HEADS * HD), D ** -0.5, 0.109375, ((2, 2),))
    space_out = heavy_noise(arg_keys[3], (HEADS * HD, D), (HEADS * HD) ** -0.5, 0.375, ((0, 2),), (0, 1, 2, 2.0))
    space_mod = draw_space_mod(jax.random.fold_in(arg_keys[8], 71), 0)
    time_qkv = scatter_about(arg_keys[5], (D, 3, HEADS * HD), D ** -0.5, 0.109375, ((2, 2),))
    time_out = heavy_noise(arg_keys[6], (HEADS * HD, D), (HEADS * HD) ** -0.5, 0.375, ((0, 2),), (0, 1, 2, 2.0))
    time_mod = draw_time_mod(jax.random.fold_in(arg_keys[8], 71), 0)
    return dict(tokens=tokens, block_mask=block_mask, space_qkv=space_qkv, space_out=space_out, space_mod=space_mod, time_qkv=time_qkv, time_out=time_out, time_mod=time_mod)


EPS = 1e-06

def modulate(stream, modulation):
    values = stream.astype(jnp.float32)
    centre = lax.optimization_barrier(jnp.mean(values, axis=-1, keepdims=True))
    centred = values - centre
    variance = lax.optimization_barrier(jnp.mean(centred * centred, axis=-1, keepdims=True))
    normed = centred * lax.rsqrt(variance + EPS)
    return (normed * (1.0 + modulation[1]) + modulation[0]).astype(jnp.bfloat16)

def softmax_rounded(scores, reduce_axis):
    row_max = lax.optimization_barrier(jnp.max(scores, axis=reduce_axis, keepdims=True))
    lifted = jnp.exp(scores - row_max)
    return (lifted / lax.optimization_barrier(jnp.sum(lifted, axis=reduce_axis, keepdims=True))).astype(jnp.bfloat16)

def out_project(attended, weight):
    group_width = attended.shape[1] // N_FSDP
    running = jnp.zeros((attended.shape[0], weight.shape[1]), jnp.float32)
    for member in range(N_FSDP):
        rounded = jnp.dot(attended[:, member * group_width:(member + 1) * group_width], weight[member * group_width:(member + 1) * group_width], preferred_element_type=jnp.float32).astype(jnp.bfloat16)
        running = running + lax.optimization_barrier(rounded).astype(jnp.float32)
    return running

def spatial_attention(packed, block_mask):
    score_scale = 1.0 / math.sqrt(HD)

    def one_frame(inputs):
        packed_frame, mask_frame = inputs
        queries = packed_frame[:, :, 0].astype(jnp.float32)
        keys_all = packed_frame[:, :, 1].astype(jnp.float32)
        values_all = packed_frame[:, :, 2].astype(jnp.float32)
        scores = jnp.einsum('bqhd,bkhd->bhqk', queries, keys_all) * score_scale
        allowed = jnp.repeat(jnp.repeat(mask_frame == 1, BLOCK, axis=0), BLOCK, axis=1)
        scores = jnp.where(allowed[None, None], scores, -jnp.inf)
        weights_bf = softmax_rounded(scores, 3)
        return jnp.einsum('bhqk,bkhd->bqhd', weights_bf.astype(jnp.float32), values_all).astype(jnp.bfloat16)
    framed = jnp.moveaxis(packed, 1, 0)
    attended = lax.map(one_frame, (framed, block_mask))
    return jnp.moveaxis(attended, 0, 1)

def temporal_attention(packed):
    score_scale = 1.0 / math.sqrt(HD)
    queries = packed[:, :, :, 0].astype(jnp.float32)
    keys_all = packed[:, :, :, 1].astype(jnp.float32)
    values_all = packed[:, :, :, 2].astype(jnp.float32)
    scores = jnp.einsum('bfphd,bgphd->bphfg', queries, keys_all) * score_scale
    weights_bf = softmax_rounded(scores, 4)
    return jnp.einsum('bphfg,bgphd->bfphd', weights_bf.astype(jnp.float32), values_all).astype(jnp.bfloat16)

def sublayer_inputs(stream_flat, qkv_weight, modulation):
    normed = modulate(stream_flat, modulation)
    packed = jnp.dot(normed, qkv_weight.reshape(D, -1), preferred_element_type=jnp.float32)
    return packed.astype(jnp.bfloat16).reshape(VIDEOS, F, P_SIZE, 3, HEADS, HD)

def reference(tokens, block_mask, space_qkv, space_out, space_mod, time_qkv, time_out, time_mod):
    heads_width = HEADS * HD
    flat_tokens = tokens.reshape(-1, D).astype(jnp.float32)
    packed = sublayer_inputs(flat_tokens, space_qkv, space_mod)
    attended = spatial_attention(packed, block_mask).reshape(-1, heads_width)
    summed = out_project(attended, space_out)
    stream = flat_tokens + space_mod[2] * summed
    packed_time = sublayer_inputs(stream, time_qkv, time_mod)
    attended_time = temporal_attention(packed_time).reshape(-1, heads_width)
    summed_time = out_project(attended_time, time_out)
    result = stream + time_mod[2] * summed_time
    return result.reshape(VIDEOS, TOKV, D)
```

```python
import functools
import math

import jax
import jax.numpy as jnp
from jax import lax
from jax.experimental import pallas as pl
from jax.experimental.pallas import tpu as pltpu
from jax.sharding import PartitionSpec as P

HD = 128
BLOCK = 128
EPS = 1e-06
GROUP = 4
MESH = pl.DeviceIdType.MESH
NT = (((1,), (1,)), ((), ()))


def softmax_rounded(scores):
    row_max = jnp.max(scores, axis=1, keepdims=True)
    lifted = jnp.exp(scores - row_max)
    return (lifted / jnp.sum(lifted, axis=1, keepdims=True)).astype(jnp.bfloat16)


def sublayers(
    sizes,
    mask_ref, tokens_ref, space_qkv_ref, space_out_ref, space_mod_ref, time_qkv_ref, time_out_ref,
    time_mod_ref, result_ref,
    stream, cols, total, queries, keys_values, mixed, sent_qkv, got_qkv, sent_att,
    qkv_w, out_w, mods, stats, normed, att_space, att_time,
    in_sem, w_sem, o_sem, m_sem, out_sem,
    stat_s, stat_r, h_s, h_r, kv_s, kv_r, as_s, as_r, at_s, at_r, wq_s, wq_r, wf_s, wf_r,
    tq_s, tq_r, ta_s, ta_r,
):
    frames, parts, rows, part_width, heads_width, chunk = sizes
    chunks = rows // chunk
    piece = rows // frames
    per_chunk = chunk // piece
    query_blocks = rows // BLOCK
    local_heads = heads_width // HD
    width = part_width * parts
    quarter = heads_width // GROUP
    scale = 1.0 / math.sqrt(HD)

    seq = lax.axis_index("seq")
    me = lax.axis_index("fsdp")
    half = lax.rem(seq, 2)
    frame = seq // 2
    member = lax.rem(seq, GROUP)
    group = seq - member

    def peer(distance):
        return lax.rem(me + distance, parts)

    def source(distance):
        return lax.rem(me + parts - distance, parts)

    def fsdp_copy(src, dst, send, recv, distance):
        return pltpu.make_async_remote_copy(
            src_ref=src, dst_ref=dst, send_sem=send, recv_sem=recv,
            device_id={"fsdp": peer(distance)}, device_id_type=MESH,
        )

    def seq_copy(src, dst, send, recv, target):
        return pltpu.make_async_remote_copy(
            src_ref=src, dst_ref=dst, send_sem=send, recv_sem=recv,
            device_id={"seq": target}, device_id_type=MESH,
        )

    qkv_refs = (space_qkv_ref, time_qkv_ref)
    out_refs = (space_out_ref, time_out_ref)
    mod_refs = (space_mod_ref, time_mod_ref)
    own_columns = pl.ds(pl.multiple_of(me * part_width, 128), part_width)

    def load_tokens():
        return pltpu.make_async_copy(tokens_ref.at[0], stream, in_sem)

    def load_qkv(layer):
        return pltpu.make_async_copy(qkv_refs[layer], qkv_w.at[layer], w_sem.at[layer])

    def load_out(layer):
        return pltpu.make_async_copy(
            out_refs[layer].at[:, own_columns], out_w.at[layer, me], o_sem.at[layer]
        )

    def load_mod(layer):
        return pltpu.make_async_copy(
            mod_refs[layer].at[:, own_columns], mods.at[layer], m_sem.at[layer]
        )

    load_tokens().start()
    for layer in range(2):
        load_mod(layer).start()
    load_qkv(0).start()
    load_out(0).start()

    barrier = pltpu.get_barrier_semaphore()
    for distance in range(1, parts):
        pl.semaphore_signal(barrier, inc=1, device_id={"fsdp": peer(distance)}, device_id_type=MESH)
    for distance in range(1, frames):
        other = lax.rem(frame + distance, frames) * 2 + half
        pl.semaphore_signal(barrier, inc=1, device_id={"seq": other}, device_id_type=MESH)
    for distance in range(GROUP // 2):
        other = group + lax.rem(member + 1 + 2 * distance, GROUP)
        pl.semaphore_signal(barrier, inc=1, device_id={"seq": other}, device_id_type=MESH)
    pl.semaphore_wait(barrier, parts - 1 + frames - 1 + GROUP // 2)

    own_quarter = pl.ds(pl.multiple_of(member * quarter, 16), quarter)

    def weight_copy(layer, distance):
        target = peer(distance)
        columns = pl.ds(pl.multiple_of(target * part_width, 128), part_width)
        return fsdp_copy(
            out_refs[layer].at[own_quarter, columns], out_w.at[layer, me, own_quarter],
            wq_s.at[layer, distance], wq_r.at[layer, distance], distance,
        )

    def spread_copy(layer, distance, step):
        block = out_w.at[layer, source(distance), own_quarter]
        return seq_copy(
            block, block, wf_s.at[layer, distance, step], wf_r.at[layer, distance, step],
            group + lax.rem(member + step, GROUP),
        )

    def arrived_spread(layer, distance, step):
        first = lax.rem(member + GROUP - step, GROUP) * quarter
        block = out_w.at[layer, source(distance), pl.ds(pl.multiple_of(first, 16), quarter)]
        return seq_copy(
            block, block, wf_s.at[layer, distance, step], wf_r.at[layer, distance, step],
            group + lax.rem(member + step, GROUP),
        )

    def send_weights(layer):
        for distance in range(1, parts):
            weight_copy(layer, distance).start()

    def spread_weights(layer):
        for distance in range(1, parts):
            weight_copy(layer, distance).wait_recv()
            for step in range(1, GROUP):
                spread_copy(layer, distance, step).start()

    def finish_weights(layer):
        load_out(layer).wait()
        for distance in range(1, parts):
            for step in range(1, GROUP):
                arrived_spread(layer, distance, step).wait_recv()

    def note_statistics(values, start, count):
        centre = jnp.sum(values, axis=1, keepdims=True) * (1.0 / part_width)
        offset = values - centre
        spread = jnp.sum(offset * offset, axis=1, keepdims=True)
        lane = lax.broadcasted_iota(jnp.int32, (count, 128), 1)
        cols[pl.ds(start, count), :] = jnp.where(lane == 0, centre, spread)

    def stat_copy(layer, distance):
        return fsdp_copy(
            stats.at[layer, me], stats.at[layer, me],
            stat_s.at[layer, distance], stat_r.at[layer, distance], distance,
        )

    def send_statistics(layer):
        stats[layer, me] = jnp.transpose(cols[...])[:8]
        for distance in range(1, parts):
            stat_copy(layer, distance).start()

    def finish_statistics(layer):
        for distance in range(1, parts):
            stat_copy(layer, distance).wait_recv()
        centre = jnp.zeros((1, rows), jnp.float32)
        for part in range(parts):
            centre = centre + stats[layer, part][0:1]
        centre = centre * (1.0 / parts)
        spread = jnp.zeros((1, rows), jnp.float32)
        for part in range(parts):
            shift = stats[layer, part][0:1] - centre
            spread = spread + stats[layer, part][1:2] * (1.0 / part_width) + shift * shift
        inverse = lax.rsqrt(spread * (1.0 / parts) + EPS)
        line = lax.broadcasted_iota(jnp.int32, (128, rows), 0)
        cols[...] = jnp.transpose(jnp.where(line == 0, centre, inverse))

    def chunk_rows(index):
        return pl.ds(pl.multiple_of(index * chunk, chunk), chunk)

    def block_rows(index):
        return pl.ds(pl.multiple_of(index * BLOCK, BLOCK), BLOCK)

    def h_copy(layer, index, distance):
        block = normed.at[layer, me, chunk_rows(index)]
        return fsdp_copy(
            block, block, h_s.at[layer, distance, index], h_r.at[layer, distance, index], distance
        )

    def send_normed(layer, order):
        shift = mods[layer, 0:1]
        gain = 1.0 + mods[layer, 1:2]

        def step(i, carry):
            index = order(i)
            span = chunk_rows(index)
            values = stream[span, :]
            line = cols[span, :]
            out = (values - line[:, 0:1]) * line[:, 1:2] * gain + shift
            normed[layer, me, span, :] = out.astype(jnp.bfloat16)
            for distance in range(1, parts):
                h_copy(layer, index, distance).start()
            return carry

        lax.fori_loop(0, chunks, step, 0)

    def own_product(layer):
        depth = pl.ds(pl.multiple_of(me * part_width, 128), part_width)

        def step(index, carry):
            span = block_rows(index)
            total[span, :] = jnp.dot(
                normed[layer, me, span, :], qkv_w[layer, depth, :],
                preferred_element_type=jnp.float32,
            )
            return carry

        lax.fori_loop(0, query_blocks, step, 0)

    def chunk_product(layer, index):
        span = chunk_rows(index)
        value = total[span, :]
        for distance in range(1, parts):
            other = source(distance)
            depth = pl.ds(pl.multiple_of(other * part_width, 128), part_width)
            value = value + jnp.dot(
                normed[layer, other, span, :], qkv_w[layer, depth, :],
                preferred_element_type=jnp.float32,
            )
        return value

    def wait_chunk(layer, index):
        for distance in range(1, parts):
            h_copy(layer, index, distance).wait_recv()

    load_tokens().wait()

    def first_statistics(i, carry):
        start = pl.multiple_of(i * chunk, chunk)
        note_statistics(stream[pl.ds(start, chunk), :], start, chunk)
        return carry

    lax.fori_loop(0, chunks, first_statistics, 0)
    send_statistics(0)
    send_weights(0)
    for layer in range(2):
        load_mod(layer).wait()
    load_qkv(1).start()
    load_out(1).start()
    finish_statistics(0)
    send_normed(0, lambda i: i)
    send_weights(1)
    load_qkv(0).wait()
    own_product(0)
    spread_weights(0)

    def kv_copy(index):
        block = keys_values.at[half, :, chunk_rows(index)]
        return seq_copy(block, block, kv_s.at[index], kv_r.at[index], seq + 1 - 2 * half)

    def space_chunk(index, carry):
        wait_chunk(0, index)
        span = chunk_rows(index)
        value = chunk_product(0, index).astype(jnp.bfloat16)
        queries[span, :] = value[:, :heads_width]
        for kind in range(2):
            first = (kind + 1) * heads_width
            keys_values[half, kind, span, :] = value[:, first:first + heads_width]
        kv_copy(index).start()
        return carry

    lax.fori_loop(0, chunks, space_chunk, 0)
    spread_weights(1)

    def wait_keys(index, carry):
        kv_copy(index).wait_recv()
        return carry

    lax.fori_loop(0, chunks, wait_keys, 0)

    def att_space_copy(index, distance):
        block = att_space.at[me, block_rows(index)]
        return fsdp_copy(
            block, block, as_s.at[distance, index], as_r.at[distance, index], distance
        )

    def space_attention(index, carry):
        span = block_rows(index)
        bias = []
        for key_block in range(2 * query_blocks):
            kept = mask_ref[frame, half * query_blocks + index, key_block]
            bias.append(jnp.full((1, BLOCK), jnp.where(kept == 1, 0.0, -jnp.inf), jnp.float32))
        bias = jnp.concatenate(bias, axis=1)
        for head in range(local_heads):
            lanes = slice(head * HD, (head + 1) * HD)
            keys = keys_values[:, 0, :, lanes].reshape(2 * rows, HD)
            values = keys_values[:, 1, :, lanes].reshape(2 * rows, HD)
            scores = lax.dot_general(
                queries[span, lanes], keys, NT, preferred_element_type=jnp.float32
            )
            weights = softmax_rounded(scores * scale + bias)
            att_space[me, span, lanes] = jnp.dot(
                weights, values, preferred_element_type=jnp.float32
            ).astype(jnp.bfloat16)
        for distance in range(1, parts):
            att_space_copy(index, distance).start()
        return carry

    lax.fori_loop(0, query_blocks, space_attention, 0)
    finish_weights(0)

    def space_project(index, carry):
        span = block_rows(index)
        for distance in range(1, parts):
            att_space_copy(index, distance).wait_recv()
        summed = jnp.zeros((BLOCK, part_width), jnp.float32)
        for part in range(parts):
            summed = summed + jnp.dot(
                att_space[part, span, :], out_w[0, part], preferred_element_type=jnp.float32
            ).astype(jnp.bfloat16).astype(jnp.float32)
        values = stream[span, :] + mods[0, 2:3] * summed
        stream[span, :] = values
        note_statistics(values, pl.multiple_of(index * BLOCK, BLOCK), BLOCK)
        return carry

    lax.fori_loop(0, query_blocks, space_project, 0)

    send_statistics(1)
    load_qkv(1).wait()
    finish_statistics(1)

    def time_order(i):
        return lax.rem(frame // per_chunk + 1 + i, chunks)

    send_normed(1, time_order)
    own_product(1)

    def tq_copy(target):
        return seq_copy(
            sent_qkv.at[target], got_qkv.at[frame], tq_s.at[target], tq_r.at[frame],
            target * 2 + half,
        )

    def tq_arrival(origin):
        return seq_copy(
            sent_qkv.at[origin], got_qkv.at[origin], tq_s.at[origin], tq_r.at[origin],
            origin * 2 + half,
        )

    def time_chunk(i, carry):
        index = time_order(i)
        wait_chunk(1, index)
        whole = chunk_product(1, index).reshape(per_chunk, piece, 3 * heads_width)
        whole = whole.astype(jnp.bfloat16)
        for n in range(per_chunk):
            target = index * per_chunk + n
            sent_qkv[target] = whole[n]

            @pl.when(target != frame)
            def _():
                tq_copy(target).start()

        return carry

    lax.fori_loop(0, chunks, time_chunk, 0)
    got_qkv[frame] = sent_qkv[frame]

    def others(action):
        def step(i, carry):
            action(lax.rem(frame + frames - 1 - i, frames))
            return carry

        lax.fori_loop(0, frames - 1, step, 0)

    others(lambda origin: tq_arrival(origin).wait_recv())

    def position(index):
        passed = jnp.zeros_like(index)
        for n in range(1, frames):
            passed = passed + jnp.where(index >= n * piece, piece, 0)
        return index - passed

    def flat(first):
        return got_qkv[:, :, first:first + HD].astype(jnp.float32).reshape(rows, HD).astype(jnp.bfloat16)

    column = position(lax.broadcasted_iota(jnp.int32, (1, rows), 1))
    for head in range(local_heads):
        first = head * HD
        head_queries = flat(first)
        head_keys = flat(heads_width + first)
        head_values = flat(2 * heads_width + first)
        for block in range(query_blocks):
            span = slice(block * BLOCK, (block + 1) * BLOCK)
            line = position(lax.broadcasted_iota(jnp.int32, (BLOCK, 1), 0) + block * BLOCK)
            scores = lax.dot_general(
                head_queries[span], head_keys, NT, preferred_element_type=jnp.float32
            ) * scale
            weights = softmax_rounded(jnp.where(line == column, scores, -jnp.inf))
            mixed[span, first:first + HD] = jnp.dot(
                weights, head_values, preferred_element_type=jnp.float32
            )
    sent_att[...] = mixed[...].reshape(frames, piece, heads_width).astype(jnp.bfloat16)
    att_time[me, frame] = sent_att[frame]

    def ta_copy(target):
        return seq_copy(
            sent_att.at[target], att_time.at[me, frame], ta_s.at[target], ta_r.at[frame],
            target * 2 + half,
        )

    def ta_arrival(origin):
        return seq_copy(
            sent_att.at[origin], att_time.at[me, origin], ta_s.at[origin], ta_r.at[origin],
            origin * 2 + half,
        )

    def send_att(i, carry):
        ta_copy(lax.rem(frame + 1 + i, frames)).start()
        return carry

    lax.fori_loop(0, frames - 1, send_att, 0)

    def att_time_copy(index, distance):
        block = att_time.at[me, index]
        return fsdp_copy(
            block, block, at_s.at[distance, index], at_r.at[distance, index], distance
        )

    def forward(index):
        for distance in range(1, parts):
            att_time_copy(index, distance).start()

    forward(frame)

    def relay(origin):
        ta_arrival(origin).wait_recv()
        forward(origin)

    others(relay)
    finish_weights(1)

    def result_copy(index):
        span = chunk_rows(index)
        return pltpu.make_async_copy(stream.at[span], result_ref.at[0, span], out_sem.at[index])

    def time_project(i, carry):
        index = lax.rem(frame // per_chunk + chunks - i, chunks)
        span = chunk_rows(index)
        for n in range(per_chunk):
            for distance in range(1, parts):
                att_time_copy(index * per_chunk + n, distance).wait_recv()
        summed = jnp.zeros((chunk, part_width), jnp.float32)
        for part in range(parts):
            attended = att_time[part, pl.ds(index * per_chunk, per_chunk)].astype(jnp.float32)
            summed = summed + jnp.dot(
                attended.reshape(chunk, heads_width).astype(jnp.bfloat16), out_w[1, part],
                preferred_element_type=jnp.float32,
            ).astype(jnp.bfloat16).astype(jnp.float32)
        stream[span, :] = stream[span, :] + mods[1, 2:3] * summed
        result_copy(index).start()
        return carry

    lax.fori_loop(0, chunks, time_project, 0)

    def drain(i, carry):
        kv_copy(i).wait_send()
        for layer in range(2):
            for distance in range(1, parts):
                h_copy(layer, i, distance).wait_send()
        result_copy(i).wait()
        return carry

    lax.fori_loop(0, chunks, drain, 0)

    def drain_blocks(i, carry):
        for distance in range(1, parts):
            att_space_copy(i, distance).wait_send()
        return carry

    lax.fori_loop(0, query_blocks, drain_blocks, 0)

    def drain_pieces(i, carry):
        for distance in range(1, parts):
            att_time_copy(i, distance).wait_send()
        return carry

    lax.fori_loop(0, frames, drain_pieces, 0)

    def drain_other(target):
        tq_copy(target).wait_send()
        ta_copy(target).wait_send()

    others(drain_other)
    for layer in range(2):
        for distance in range(1, parts):
            stat_copy(layer, distance).wait_send()
            weight_copy(layer, distance).wait_send()
            for step in range(1, GROUP):
                spread_copy(layer, distance, step).wait_send()


def on_device(tokens, block_mask, space_qkv, space_out, space_mod, time_qkv, time_out, time_mod):
    videos, rows, part_width = tokens.shape
    heads_width = space_qkv.shape[2]
    frames = lax.axis_size("seq") // 2
    parts = lax.axis_size("fsdp")
    piece = rows // frames
    chunk = piece if piece % 16 == 0 else 2 * piece
    chunks = rows // chunk
    blocks = rows // BLOCK
    width = part_width * parts
    bf16, f32 = jnp.bfloat16, jnp.float32
    dma = pltpu.SemaphoreType.DMA
    hbm = pl.BlockSpec(memory_space=pl.ANY)
    scratch = [
        pltpu.VMEM((rows, part_width), f32),
        pltpu.VMEM((rows, 128), f32),
        pltpu.VMEM((rows, 3 * heads_width), f32),
        pltpu.VMEM((rows, heads_width), bf16),
        pltpu.VMEM((2, 2, rows, heads_width), bf16),
        pltpu.VMEM((rows, heads_width), f32),
        pltpu.VMEM((frames, piece, 3 * heads_width), bf16),
        pltpu.VMEM((frames, piece, 3 * heads_width), bf16),
        pltpu.VMEM((frames, piece, heads_width), bf16),
        pltpu.VMEM((2, width, 3 * heads_width), bf16),
        pltpu.VMEM((2, parts, heads_width, part_width), bf16),
        pltpu.VMEM((2, 3, part_width), f32),
        pltpu.VMEM((2, parts, 8, rows), f32),
        pltpu.VMEM((2, parts, rows, part_width), bf16),
        pltpu.VMEM((parts, rows, heads_width), bf16),
        pltpu.VMEM((parts, frames, piece, heads_width), bf16),
        dma, dma((2,)), dma((2,)), dma((2,)), dma((chunks,)),
        dma((2, parts)), dma((2, parts)),
        dma((2, parts, chunks)), dma((2, parts, chunks)),
        dma((chunks,)), dma((chunks,)),
        dma((parts, blocks)), dma((parts, blocks)),
        dma((parts, frames)), dma((parts, frames)),
        dma((2, parts)), dma((2, parts)),
        dma((2, parts, GROUP)), dma((2, parts, GROUP)),
        dma((frames,)), dma((frames,)),
        dma((frames,)), dma((frames,)),
    ]
    sizes = (frames, parts, rows, part_width, heads_width, chunk)
    return pl.pallas_call(
        functools.partial(sublayers, sizes),
        out_shape=jax.ShapeDtypeStruct(tokens.shape, f32),
        in_specs=[pl.BlockSpec(memory_space=pltpu.SMEM)] + [hbm] * 7,
        out_specs=hbm,
        scratch_shapes=scratch,
        compiler_params=pltpu.CompilerParams(
            collective_id=0, has_side_effects=True, vmem_limit_bytes=52 * 1024 * 1024
        ),
        cost_estimate=pl.CostEstimate(
            flops=4 * rows * width * 4 * heads_width, bytes_accessed=20 * 1024 * 1024,
            transcendentals=1024 * 1024,
        ),
    )(
        block_mask, tokens, space_qkv.reshape(width, -1), space_out, space_mod,
        time_qkv.reshape(width, -1), time_out, time_mod,
    )


def solution(mesh):
    placed = (
        P(None, "seq", "fsdp"),
        P(),
        P(None, None, "fsdp"),
        P("fsdp", None),
        P(),
        P(None, None, "fsdp"),
        P("fsdp", None),
        P(),
    )
    return jax.shard_map(
        on_device, mesh=mesh, in_specs=placed, out_specs=P(None, "seq", "fsdp"), check_vma=False
    )
```

```python
import functools
import math

import jax
import jax.numpy as jnp
from jax import lax
from jax.experimental import pallas as pl
from jax.experimental.pallas import tpu as pltpu
from jax.sharding import PartitionSpec as P

HD = 128
BLOCK = 128
EPS = 1e-06
GROUP = 4
MESH = pl.DeviceIdType.MESH
NT = (((1,), (1,)), ((), ()))


def softmax_rounded(scores):
    row_max = jnp.max(scores, axis=1, keepdims=True)
    lifted = jnp.exp(scores - row_max)
    return (lifted / jnp.sum(lifted, axis=1, keepdims=True)).astype(jnp.bfloat16)


def sublayers(
    sizes,
    mask_ref, tokens_ref, space_qkv_ref, space_out_ref, space_mod_ref, time_qkv_ref, time_out_ref,
    time_mod_ref, result_ref,
    stream, cols, total, queries, keys_values, mixed, sent_qkv, got_qkv, sent_att,
    qkv_w, out_w, mods, stats, normed, att_space, att_time,
    in_sem, w_sem, o_sem, m_sem, out_sem,
    stat_s, stat_r, h_s, h_r, kv_s, kv_r, as_s, as_r, at_s, at_r, wq_s, wq_r, wf_s, wf_r,
    tq_s, tq_r, ta_s, ta_r,
):
    frames, parts, rows, part_width, heads_width, chunk = sizes
    chunks = rows // chunk
    piece = rows // frames
    per_chunk = chunk // piece
    query_blocks = rows // BLOCK
    local_heads = heads_width // HD
    width = part_width * parts
    quarter = heads_width // GROUP
    scale = 1.0 / math.sqrt(HD)

    seq = lax.axis_index("seq")
    me = lax.axis_index("fsdp")
    half = lax.rem(seq, 2)
    frame = seq // 2
    member = lax.rem(seq, GROUP)
    group = seq - member

    def peer(distance):
        return lax.rem(me + distance, parts)

    def source(distance):
        return lax.rem(me + parts - distance, parts)

    def fsdp_copy(src, dst, send, recv, distance):
        return pltpu.make_async_remote_copy(
            src_ref=src, dst_ref=dst, send_sem=send, recv_sem=recv,
            device_id={"fsdp": peer(distance)}, device_id_type=MESH,
        )

    def seq_copy(src, dst, send, recv, target):
        return pltpu.make_async_remote_copy(
            src_ref=src, dst_ref=dst, send_sem=send, recv_sem=recv,
            device_id={"seq": target}, device_id_type=MESH,
        )

    qkv_refs = (space_qkv_ref, time_qkv_ref)
    out_refs = (space_out_ref, time_out_ref)
    mod_refs = (space_mod_ref, time_mod_ref)
    own_columns = pl.ds(pl.multiple_of(me * part_width, 128), part_width)

    def load_tokens():
        return pltpu.make_async_copy(tokens_ref.at[0], stream, in_sem)

    def load_qkv(layer, kind):
        lanes = pl.ds(kind * heads_width, heads_width)
        return pltpu.make_async_copy(
            qkv_refs[layer].at[kind], qkv_w.at[layer, :, lanes], w_sem.at[layer, kind]
        )

    def load_out(layer):
        return pltpu.make_async_copy(
            out_refs[layer].at[:, own_columns], out_w.at[layer, me], o_sem.at[layer]
        )

    def load_mod(layer):
        return pltpu.make_async_copy(
            mod_refs[layer].at[:, own_columns], mods.at[layer], m_sem.at[layer]
        )

    load_tokens().start()
    for layer in range(2):
        load_mod(layer).start()
    for kind in range(3):
        load_qkv(0, kind).start()
    load_out(0).start()

    barrier = pltpu.get_barrier_semaphore()
    for distance in range(1, parts):
        pl.semaphore_signal(barrier, inc=1, device_id={"fsdp": peer(distance)}, device_id_type=MESH)
    for distance in range(1, frames):
        other = lax.rem(frame + distance, frames) * 2 + half
        pl.semaphore_signal(barrier, inc=1, device_id={"seq": other}, device_id_type=MESH)
    for distance in range(GROUP // 2):
        other = group + lax.rem(member + 1 + 2 * distance, GROUP)
        pl.semaphore_signal(barrier, inc=1, device_id={"seq": other}, device_id_type=MESH)
    pl.semaphore_wait(barrier, parts - 1 + frames - 1 + GROUP // 2)

    own_quarter = pl.ds(pl.multiple_of(member * quarter, 16), quarter)

    def weight_copy(layer, distance):
        target = peer(distance)
        columns = pl.ds(pl.multiple_of(target * part_width, 128), part_width)
        return fsdp_copy(
            out_refs[layer].at[own_quarter, columns], out_w.at[layer, me, own_quarter],
            wq_s.at[layer, distance], wq_r.at[layer, distance], distance,
        )

    def spread_copy(layer, distance, step):
        block = out_w.at[layer, source(distance), own_quarter]
        return seq_copy(
            block, block, wf_s.at[layer, distance, step], wf_r.at[layer, distance, step],
            group + lax.rem(member + step, GROUP),
        )

    def arrived_spread(layer, distance, step):
        first = lax.rem(member + GROUP - step, GROUP) * quarter
        block = out_w.at[layer, source(distance), pl.ds(pl.multiple_of(first, 16), quarter)]
        return seq_copy(
            block, block, wf_s.at[layer, distance, step], wf_r.at[layer, distance, step],
            group + lax.rem(member + step, GROUP),
        )

    def send_weights(layer):
        for distance in range(1, parts):
            weight_copy(layer, distance).start()

    def spread_weights(layer):
        for distance in range(1, parts):
            weight_copy(layer, distance).wait_recv()
            for step in range(1, GROUP):
                spread_copy(layer, distance, step).start()

    def finish_weights(layer):
        load_out(layer).wait()
        for distance in range(1, parts):
            for step in range(1, GROUP):
                arrived_spread(layer, distance, step).wait_recv()

    def note_statistics(values, start, count):
        centre = jnp.sum(values, axis=1, keepdims=True) * (1.0 / part_width)
        offset = values - centre
        spread = jnp.sum(offset * offset, axis=1, keepdims=True)
        lane = lax.broadcasted_iota(jnp.int32, (count, 128), 1)
        cols[pl.ds(start, count), :] = jnp.where(lane == 0, centre, spread)

    def stat_copy(layer, distance):
        return fsdp_copy(
            stats.at[layer, me], stats.at[layer, me],
            stat_s.at[layer, distance], stat_r.at[layer, distance], distance,
        )

    def send_statistics(layer):
        stats[layer, me] = jnp.transpose(cols[...])[:8]
        for distance in range(1, parts):
            stat_copy(layer, distance).start()

    def finish_statistics(layer):
        for distance in range(1, parts):
            stat_copy(layer, distance).wait_recv()
        centre = jnp.zeros((1, rows), jnp.float32)
        for part in range(parts):
            centre = centre + stats[layer, part][0:1]
        centre = centre * (1.0 / parts)
        spread = jnp.zeros((1, rows), jnp.float32)
        for part in range(parts):
            shift = stats[layer, part][0:1] - centre
            spread = spread + stats[layer, part][1:2] * (1.0 / part_width) + shift * shift
        inverse = lax.rsqrt(spread * (1.0 / parts) + EPS)
        line = lax.broadcasted_iota(jnp.int32, (128, rows), 0)
        cols[...] = jnp.transpose(jnp.where(line == 0, centre, inverse))

    def chunk_rows(index):
        return pl.ds(pl.multiple_of(index * chunk, chunk), chunk)

    def block_rows(index):
        return pl.ds(pl.multiple_of(index * BLOCK, BLOCK), BLOCK)

    def h_copy(layer, index, distance):
        block = normed.at[layer, me, chunk_rows(index)]
        return fsdp_copy(
            block, block, h_s.at[layer, distance, index], h_r.at[layer, distance, index], distance
        )

    def send_normed(layer, order):
        shift = mods[layer, 0:1]
        gain = 1.0 + mods[layer, 1:2]

        def step(i, carry):
            index = order(i)
            span = chunk_rows(index)
            values = stream[span, :]
            line = cols[span, :]
            out = (values - line[:, 0:1]) * line[:, 1:2] * gain + shift
            normed[layer, me, span, :] = out.astype(jnp.bfloat16)
            for distance in range(1, parts):
                h_copy(layer, index, distance).start()
            return carry

        lax.fori_loop(0, chunks, step, 0)

    def own_product(layer):
        depth = pl.ds(pl.multiple_of(me * part_width, 128), part_width)

        def step(index, carry):
            span = block_rows(index)
            total[span, :] = jnp.dot(
                normed[layer, me, span, :], qkv_w[layer, depth, :],
                preferred_element_type=jnp.float32,
            )
            return carry

        lax.fori_loop(0, query_blocks, step, 0)

    def chunk_product(layer, index):
        span = chunk_rows(index)
        value = total[span, :]
        for distance in range(1, parts):
            other = source(distance)
            depth = pl.ds(pl.multiple_of(other * part_width, 128), part_width)
            value = value + jnp.dot(
                normed[layer, other, span, :], qkv_w[layer, depth, :],
                preferred_element_type=jnp.float32,
            )
        return value

    def wait_chunk(layer, index):
        for distance in range(1, parts):
            h_copy(layer, index, distance).wait_recv()

    load_tokens().wait()

    def first_statistics(i, carry):
        start = pl.multiple_of(i * chunk, chunk)
        note_statistics(stream[pl.ds(start, chunk), :], start, chunk)
        return carry

    lax.fori_loop(0, chunks, first_statistics, 0)
    send_statistics(0)
    send_weights(0)
    for layer in range(2):
        load_mod(layer).wait()
    for kind in range(3):
        load_qkv(1, kind).start()
    load_out(1).start()
    finish_statistics(0)
    send_normed(0, lambda i: i)
    send_weights(1)
    for kind in range(3):
        load_qkv(0, kind).wait()
    own_product(0)
    spread_weights(0)

    def kv_copy(index):
        block = keys_values.at[half, :, chunk_rows(index)]
        return seq_copy(block, block, kv_s.at[index], kv_r.at[index], seq + 1 - 2 * half)

    def space_chunk(index, carry):
        wait_chunk(0, index)
        span = chunk_rows(index)
        value = chunk_product(0, index).astype(jnp.bfloat16)
        queries[span, :] = value[:, :heads_width]
        for kind in range(2):
            first = (kind + 1) * heads_width
            keys_values[half, kind, span, :] = value[:, first:first + heads_width]
        kv_copy(index).start()
        return carry

    lax.fori_loop(0, chunks, space_chunk, 0)
    spread_weights(1)

    def wait_keys(index, carry):
        kv_copy(index).wait_recv()
        return carry

    lax.fori_loop(0, chunks, wait_keys, 0)

    def att_space_copy(index, distance):
        block = att_space.at[me, block_rows(index)]
        return fsdp_copy(
            block, block, as_s.at[distance, index], as_r.at[distance, index], distance
        )

    def space_attention(index, carry):
        span = block_rows(index)
        bias = []
        for key_block in range(2 * query_blocks):
            kept = mask_ref[frame, half * query_blocks + index, key_block]
            bias.append(jnp.full((1, BLOCK), jnp.where(kept == 1, 0.0, -jnp.inf), jnp.float32))
        bias = jnp.concatenate(bias, axis=1)
        for head in range(local_heads):
            lanes = slice(head * HD, (head + 1) * HD)
            keys = keys_values[:, 0, :, lanes].reshape(2 * rows, HD)
            values = keys_values[:, 1, :, lanes].reshape(2 * rows, HD)
            scores = lax.dot_general(
                queries[span, lanes], keys, NT, preferred_element_type=jnp.float32
            )
            weights = softmax_rounded(scores * scale + bias)
            att_space[me, span, lanes] = jnp.dot(
                weights, values, preferred_element_type=jnp.float32
            ).astype(jnp.bfloat16)
        for distance in range(1, parts):
            att_space_copy(index, distance).start()
        return carry

    lax.fori_loop(0, query_blocks, space_attention, 0)
    finish_weights(0)

    def space_project(index, carry):
        span = block_rows(index)
        for distance in range(1, parts):
            att_space_copy(index, distance).wait_recv()
        summed = jnp.zeros((BLOCK, part_width), jnp.float32)
        for part in range(parts):
            summed = summed + jnp.dot(
                att_space[part, span, :], out_w[0, part], preferred_element_type=jnp.float32
            ).astype(jnp.bfloat16).astype(jnp.float32)
        values = stream[span, :] + mods[0, 2:3] * summed
        stream[span, :] = values
        note_statistics(values, pl.multiple_of(index * BLOCK, BLOCK), BLOCK)
        return carry

    lax.fori_loop(0, query_blocks, space_project, 0)

    send_statistics(1)
    for kind in range(3):
        load_qkv(1, kind).wait()
    finish_statistics(1)

    def time_order(i):
        return lax.rem(frame // per_chunk + 1 + i, chunks)

    send_normed(1, time_order)
    own_product(1)

    def tq_copy(target):
        return seq_copy(
            sent_qkv.at[target], got_qkv.at[frame], tq_s.at[target], tq_r.at[frame],
            target * 2 + half,
        )

    def tq_arrival(origin):
        return seq_copy(
            sent_qkv.at[origin], got_qkv.at[origin], tq_s.at[origin], tq_r.at[origin],
            origin * 2 + half,
        )

    def time_chunk(i, carry):
        index = time_order(i)
        wait_chunk(1, index)
        whole = chunk_product(1, index).reshape(per_chunk, piece, 3 * heads_width)
        whole = whole.astype(jnp.bfloat16)
        for n in range(per_chunk):
            target = index * per_chunk + n
            sent_qkv[target] = whole[n]

            @pl.when(target != frame)
            def _():
                tq_copy(target).start()

        return carry

    lax.fori_loop(0, chunks, time_chunk, 0)
    got_qkv[frame] = sent_qkv[frame]

    def others(action):
        def step(i, carry):
            action(lax.rem(frame + frames - 1 - i, frames))
            return carry

        lax.fori_loop(0, frames - 1, step, 0)

    others(lambda origin: tq_arrival(origin).wait_recv())

    def position(index):
        passed = jnp.zeros_like(index)
        for n in range(1, frames):
            passed = passed + jnp.where(index >= n * piece, piece, 0)
        return index - passed

    def flat(first):
        return got_qkv[:, :, first:first + HD].astype(jnp.float32).reshape(rows, HD).astype(jnp.bfloat16)

    column = position(lax.broadcasted_iota(jnp.int32, (1, rows), 1))
    for head in range(local_heads):
        first = head * HD
        head_queries = flat(first)
        head_keys = flat(heads_width + first)
        head_values = flat(2 * heads_width + first)
        for block in range(query_blocks):
            span = slice(block * BLOCK, (block + 1) * BLOCK)
            line = position(lax.broadcasted_iota(jnp.int32, (BLOCK, 1), 0) + block * BLOCK)
            scores = lax.dot_general(
                head_queries[span], head_keys, NT, preferred_element_type=jnp.float32
            ) * scale
            weights = softmax_rounded(jnp.where(line == column, scores, -jnp.inf))
            mixed[span, first:first + HD] = jnp.dot(
                weights, head_values, preferred_element_type=jnp.float32
            )
    sent_att[...] = mixed[...].reshape(frames, piece, heads_width).astype(jnp.bfloat16)
    att_time[me, frame] = sent_att[frame]

    def ta_copy(target):
        return seq_copy(
            sent_att.at[target], att_time.at[me, frame], ta_s.at[target], ta_r.at[frame],
            target * 2 + half,
        )

    def ta_arrival(origin):
        return seq_copy(
            sent_att.at[origin], att_time.at[me, origin], ta_s.at[origin], ta_r.at[origin],
            origin * 2 + half,
        )

    def send_att(i, carry):
        ta_copy(lax.rem(frame + 1 + i, frames)).start()
        return carry

    lax.fori_loop(0, frames - 1, send_att, 0)

    def att_time_copy(index, distance):
        block = att_time.at[me, index]
        return fsdp_copy(
            block, block, at_s.at[distance, index], at_r.at[distance, index], distance
        )

    def forward(index):
        for distance in range(1, parts):
            att_time_copy(index, distance).start()

    forward(frame)

    def relay(origin):
        ta_arrival(origin).wait_recv()
        forward(origin)

    others(relay)
    finish_weights(1)

    def result_copy(index):
        span = chunk_rows(index)
        return pltpu.make_async_copy(stream.at[span], result_ref.at[0, span], out_sem.at[index])

    def time_project(i, carry):
        index = lax.rem(frame // per_chunk + chunks - i, chunks)
        span = chunk_rows(index)
        for n in range(per_chunk):
            for distance in range(1, parts):
                att_time_copy(index * per_chunk + n, distance).wait_recv()
        summed = jnp.zeros((chunk, part_width), jnp.float32)
        for part in range(parts):
            attended = att_time[part, pl.ds(index * per_chunk, per_chunk)].astype(jnp.float32)
            summed = summed + jnp.dot(
                attended.reshape(chunk, heads_width).astype(jnp.bfloat16), out_w[1, part],
                preferred_element_type=jnp.float32,
            ).astype(jnp.bfloat16).astype(jnp.float32)
        stream[span, :] = stream[span, :] + mods[1, 2:3] * summed
        result_copy(index).start()
        return carry

    lax.fori_loop(0, chunks, time_project, 0)

    def drain(i, carry):
        kv_copy(i).wait_send()
        for layer in range(2):
            for distance in range(1, parts):
                h_copy(layer, i, distance).wait_send()
        result_copy(i).wait()
        return carry

    lax.fori_loop(0, chunks, drain, 0)

    def drain_blocks(i, carry):
        for distance in range(1, parts):
            att_space_copy(i, distance).wait_send()
        return carry

    lax.fori_loop(0, query_blocks, drain_blocks, 0)

    def drain_pieces(i, carry):
        for distance in range(1, parts):
            att_time_copy(i, distance).wait_send()
        return carry

    lax.fori_loop(0, frames, drain_pieces, 0)

    def drain_other(target):
        tq_copy(target).wait_send()
        ta_copy(target).wait_send()

    others(drain_other)
    for layer in range(2):
        for distance in range(1, parts):
            stat_copy(layer, distance).wait_send()
            weight_copy(layer, distance).wait_send()
            for step in range(1, GROUP):
                spread_copy(layer, distance, step).wait_send()


def on_device(tokens, block_mask, space_qkv, space_out, space_mod, time_qkv, time_out, time_mod):
    videos, rows, part_width = tokens.shape
    heads_width = space_qkv.shape[2]
    frames = lax.axis_size("seq") // 2
    parts = lax.axis_size("fsdp")
    piece = rows // frames
    chunk = piece if piece % 16 == 0 else 2 * piece
    chunks = rows // chunk
    blocks = rows // BLOCK
    width = part_width * parts
    bf16, f32 = jnp.bfloat16, jnp.float32
    dma = pltpu.SemaphoreType.DMA
    hbm = pl.BlockSpec(memory_space=pl.ANY)
    scratch = [
        pltpu.VMEM((rows, part_width), f32),
        pltpu.VMEM((rows, 128), f32),
        pltpu.VMEM((rows, 3 * heads_width), f32),
        pltpu.VMEM((rows, heads_width), bf16),
        pltpu.VMEM((2, 2, rows, heads_width), bf16),
        pltpu.VMEM((rows, heads_width), f32),
        pltpu.VMEM((frames, piece, 3 * heads_width), bf16),
        pltpu.VMEM((frames, piece, 3 * heads_width), bf16),
        pltpu.VMEM((frames, piece, heads_width), bf16),
        pltpu.VMEM((2, width, 3 * heads_width), bf16),
        pltpu.VMEM((2, parts, heads_width, part_width), bf16),
        pltpu.VMEM((2, 3, part_width), f32),
        pltpu.VMEM((2, parts, 8, rows), f32),
        pltpu.VMEM((2, parts, rows, part_width), bf16),
        pltpu.VMEM((parts, rows, heads_width), bf16),
        pltpu.VMEM((parts, frames, piece, heads_width), bf16),
        dma, dma((2, 3)), dma((2,)), dma((2,)), dma((chunks,)),
        dma((2, parts)), dma((2, parts)),
        dma((2, parts, chunks)), dma((2, parts, chunks)),
        dma((chunks,)), dma((chunks,)),
        dma((parts, blocks)), dma((parts, blocks)),
        dma((parts, frames)), dma((parts, frames)),
        dma((2, parts)), dma((2, parts)),
        dma((2, parts, GROUP)), dma((2, parts, GROUP)),
        dma((frames,)), dma((frames,)),
        dma((frames,)), dma((frames,)),
    ]
    sizes = (frames, parts, rows, part_width, heads_width, chunk)
    return pl.pallas_call(
        functools.partial(sublayers, sizes),
        out_shape=jax.ShapeDtypeStruct(tokens.shape, f32),
        in_specs=[pl.BlockSpec(memory_space=pltpu.SMEM)] + [hbm] * 7,
        out_specs=hbm,
        scratch_shapes=scratch,
        compiler_params=pltpu.CompilerParams(
            collective_id=0, has_side_effects=True, vmem_limit_bytes=52 * 1024 * 1024
        ),
        cost_estimate=pl.CostEstimate(
            flops=4 * rows * width * 4 * heads_width, bytes_accessed=20 * 1024 * 1024,
            transcendentals=1024 * 1024,
        ),
    )(
        block_mask, tokens, jnp.swapaxes(space_qkv, 0, 1), space_out, space_mod,
        jnp.swapaxes(time_qkv, 0, 1), time_out, time_mod,
    )


def solution(mesh):
    placed = (
        P(None, "seq", "fsdp"),
        P(),
        P(None, None, "fsdp"),
        P("fsdp", None),
        P(),
        P(None, None, "fsdp"),
        P("fsdp", None),
        P(),
    )
    return jax.shard_map(
        on_device, mesh=mesh, in_specs=placed, out_specs=P(None, "seq", "fsdp"), check_vma=False
    )
```

```python
import functools
import math

import jax
import jax.numpy as jnp
from jax import lax
from jax.experimental import pallas as pl
from jax.experimental.pallas import tpu as pltpu
from jax.sharding import PartitionSpec as P

HD = 128
BLOCK = 128
EPS = 1e-06
RING = 8
MESH = pl.DeviceIdType.MESH
NT = (((1,), (1,)), ((), ()))


def softmax_rounded(scores):
    row_max = jnp.max(scores, axis=1, keepdims=True)
    lifted = jnp.exp(scores - row_max)
    return (lifted / jnp.sum(lifted, axis=1, keepdims=True)).astype(jnp.bfloat16)


def sublayers(
    sizes,
    mask_ref, tokens_ref, space_qkv_ref, space_out_ref, space_mod_ref, time_qkv_ref, time_out_ref,
    time_mod_ref, result_ref,
    stream, cols, total, queries, keys_values, mixed, sent_qkv, got_qkv, sent_att,
    space_w, cross_w, out_w, mods, stats, normed, h_time, part_sent, part_got, att_space, att_time,
    in_sem, w_sem, x_sem, o_sem, m_sem, out_sem,
    stat_s, stat_r, h_s, h_r, p_s, p_r, kv_s, kv_r, as_s, as_r, at_s, at_r,
    wq_s, wq_r, wf_s, wf_r, wc_s, wc_r, tq_s, tq_r, ta_s, ta_r,
):
    frames, parts, rows, part_width, heads_width, chunk = sizes
    chunks = rows // chunk
    piece = rows // frames
    per_chunk = chunk // piece
    query_blocks = rows // BLOCK
    local_heads = heads_width // HD
    width = part_width * parts
    slab = part_width // RING
    lane_count = heads_width // 2
    scale = 1.0 / math.sqrt(HD)

    seq = lax.axis_index("seq")
    me = lax.axis_index("fsdp")
    half = lax.rem(seq, 2)
    frame = seq // 2
    place = lax.rem(frame, RING)
    base = frame - place

    def peer(distance):
        return lax.rem(me + distance, parts)

    def source(distance):
        return lax.rem(me + parts - distance, parts)

    def fsdp_copy(src, dst, send, recv, distance):
        return pltpu.make_async_remote_copy(
            src_ref=src, dst_ref=dst, send_sem=send, recv_sem=recv,
            device_id={"fsdp": peer(distance)}, device_id_type=MESH,
        )

    def seq_copy(src, dst, send, recv, target):
        return pltpu.make_async_remote_copy(
            src_ref=src, dst_ref=dst, send_sem=send, recv_sem=recv,
            device_id={"seq": target}, device_id_type=MESH,
        )

    out_refs = (space_out_ref, time_out_ref)
    mod_refs = (space_mod_ref, time_mod_ref)
    own_columns = pl.ds(pl.multiple_of(me * part_width, 128), part_width)
    other_core = seq + 1 - 2 * half

    def load_tokens():
        return pltpu.make_async_copy(tokens_ref.at[0], stream, in_sem)

    def load_space(kind):
        lanes = pl.ds(kind * heads_width, heads_width)
        return pltpu.make_async_copy(
            space_qkv_ref.at[kind], space_w.at[:, lanes], w_sem.at[kind]
        )

    def load_time():
        return pltpu.make_async_copy(
            time_qkv_ref.at[:, own_columns], cross_w.at[me], x_sem
        )

    def load_out(layer):
        return pltpu.make_async_copy(
            out_refs[layer].at[:, :, :, own_columns], out_w.at[layer, me], o_sem.at[layer]
        )

    def load_mod(layer):
        return pltpu.make_async_copy(
            mod_refs[layer].at[:, own_columns], mods.at[layer], m_sem.at[layer]
        )

    load_tokens().start()
    for layer in range(2):
        load_mod(layer).start()
    for kind in range(3):
        load_space(kind).start()

    barrier = pltpu.get_barrier_semaphore()
    for distance in range(1, parts):
        pl.semaphore_signal(barrier, inc=1, device_id={"fsdp": peer(distance)}, device_id_type=MESH)
    for distance in range(1, frames):
        other = lax.rem(frame + distance, frames) * 2 + half
        pl.semaphore_signal(barrier, inc=1, device_id={"seq": other}, device_id_type=MESH)
    pl.semaphore_signal(barrier, inc=1, device_id={"seq": other_core}, device_id_type=MESH)
    pl.semaphore_wait(barrier, parts + frames - 1)

    def slab_rows(first):
        return pl.ds(pl.multiple_of(first, 16), slab)

    own_lanes = pl.ds(pl.multiple_of(half * lane_count, 128), lane_count)

    def weight_piece(kind, owner, index):
        if kind == 1:
            return cross_w.at[owner, :, slab_rows(index * slab), own_lanes]
        return out_w.at[kind // 2, owner, index, half]

    def weight_copy(kind, distance):
        target = peer(distance)
        if kind == 1:
            first = target * part_width + place * slab
            block = time_qkv_ref.at[:, slab_rows(first), own_lanes]
        else:
            columns = pl.ds(pl.multiple_of(target * part_width, 128), part_width)
            block = out_refs[kind // 2].at[place, half, :, columns]
        return fsdp_copy(
            block, weight_piece(kind, me, place),
            wq_s.at[kind, distance], wq_r.at[kind, distance], distance,
        )

    def ring_copy(kind, distance, step, index):
        block = weight_piece(kind, source(distance), index)
        return seq_copy(
            block, block, wf_s.at[kind, distance, step], wf_r.at[kind, distance, step],
            (base + lax.rem(place + step, RING)) * 2 + half,
        )

    def core_copy(kind, distance):
        owner = source(distance)
        if kind == 1:
            block = cross_w.at[owner, :, :, own_lanes]
        else:
            block = out_w.at[kind // 2, owner, :, half]
        return seq_copy(
            block, block, wc_s.at[kind, distance], wc_r.at[kind, distance], other_core
        )

    def ring_steps(action):
        def step(i, carry):
            action(i + 1)
            return carry

        lax.fori_loop(0, RING - 1, step, 0)

    def fetch_weights(kind):
        for distance in range(1, parts):
            weight_copy(kind, distance).start()

    def pass_weights(kind):
        for distance in range(1, parts):
            weight_copy(kind, distance).wait_recv()
            ring_steps(lambda step: ring_copy(kind, distance, step, place).start())

    def swap_weights(kind):
        for distance in range(1, parts):
            ring_steps(
                lambda step: ring_copy(
                    kind, distance, step, lax.rem(place + RING - step, RING)
                ).wait_recv()
            )
            core_copy(kind, distance).start()

    def finish_weights(kind):
        for distance in range(1, parts):
            core_copy(kind, distance).wait_recv()

    def out_weight(layer, part):
        return out_w[layer, part].reshape(heads_width, part_width)

    def note_statistics(values, start, count):
        centre = jnp.sum(values, axis=1, keepdims=True) * (1.0 / part_width)
        offset = values - centre
        spread = jnp.sum(offset * offset, axis=1, keepdims=True)
        lane = lax.broadcasted_iota(jnp.int32, (count, 128), 1)
        cols[pl.ds(start, count), :] = jnp.where(lane == 0, centre, spread)

    def stat_copy(layer, distance):
        return fsdp_copy(
            stats.at[layer, me], stats.at[layer, me],
            stat_s.at[layer, distance], stat_r.at[layer, distance], distance,
        )

    def send_statistics(layer):
        stats[layer, me] = jnp.transpose(cols[...])[:8]
        for distance in range(1, parts):
            stat_copy(layer, distance).start()

    def finish_statistics(layer):
        for distance in range(1, parts):
            stat_copy(layer, distance).wait_recv()
        centre = jnp.zeros((1, rows), jnp.float32)
        for part in range(parts):
            centre = centre + stats[layer, part][0:1]
        centre = centre * (1.0 / parts)
        spread = jnp.zeros((1, rows), jnp.float32)
        for part in range(parts):
            shift = stats[layer, part][0:1] - centre
            spread = spread + stats[layer, part][1:2] * (1.0 / part_width) + shift * shift
        inverse = lax.rsqrt(spread * (1.0 / parts) + EPS)
        line = lax.broadcasted_iota(jnp.int32, (128, rows), 0)
        cols[...] = jnp.transpose(jnp.where(line == 0, centre, inverse))

    def chunk_rows(index):
        return pl.ds(pl.multiple_of(index * chunk, chunk), chunk)

    def block_rows(index):
        return pl.ds(pl.multiple_of(index * BLOCK, BLOCK), BLOCK)

    def h_copy(index, distance):
        block = normed.at[me, chunk_rows(index)]
        return fsdp_copy(
            block, block, h_s.at[distance, index], h_r.at[distance, index], distance
        )

    def normalised(layer, span):
        line = cols[span, :]
        shift = mods[layer, 0:1]
        gain = 1.0 + mods[layer, 1:2]
        values = (stream[span, :] - line[:, 0:1]) * line[:, 1:2] * gain + shift
        return values.astype(jnp.bfloat16)

    load_tokens().wait()

    def first_statistics(i, carry):
        start = pl.multiple_of(i * chunk, chunk)
        note_statistics(stream[pl.ds(start, chunk), :], start, chunk)
        return carry

    lax.fori_loop(0, chunks, first_statistics, 0)
    send_statistics(0)
    for kind in range(3):
        fetch_weights(kind)
    for layer in range(2):
        load_mod(layer).wait()
    load_time().start()
    load_out(0).start()
    load_out(1).start()
    finish_statistics(0)

    def space_send(index, carry):
        span = chunk_rows(index)
        normed[me, span, :] = normalised(0, span)
        for distance in range(1, parts):
            h_copy(index, distance).start()
        return carry

    lax.fori_loop(0, chunks, space_send, 0)
    for kind in range(3):
        pass_weights(kind)
    for kind in range(3):
        load_space(kind).wait()

    def space_depth(owner):
        return pl.ds(pl.multiple_of(owner * part_width, 128), part_width)

    def space_own(index, carry):
        span = block_rows(index)
        total[span, :] = jnp.dot(
            normed[me, span, :], space_w[space_depth(me), :], preferred_element_type=jnp.float32
        )
        return carry

    lax.fori_loop(0, query_blocks, space_own, 0)

    def kv_copy(index):
        block = keys_values.at[half, :, chunk_rows(index)]
        return seq_copy(block, block, kv_s.at[index], kv_r.at[index], other_core)

    def space_chunk(index, carry):
        span = chunk_rows(index)
        value = total[span, :]
        for distance in range(1, parts):
            h_copy(index, distance).wait_recv()
            other = source(distance)
            value = value + jnp.dot(
                normed[other, span, :], space_w[space_depth(other), :],
                preferred_element_type=jnp.float32,
            )
        value = value.astype(jnp.bfloat16)
        queries[span, :] = value[:, :heads_width]
        for kind in range(2):
            first = (kind + 1) * heads_width
            keys_values[half, kind, span, :] = value[:, first:first + heads_width]
        kv_copy(index).start()
        return carry

    lax.fori_loop(0, chunks, space_chunk, 0)
    swap_weights(0)

    def wait_keys(index, carry):
        kv_copy(index).wait_recv()
        return carry

    lax.fori_loop(0, chunks, wait_keys, 0)

    def att_space_copy(index, distance):
        block = att_space.at[me, block_rows(index)]
        return fsdp_copy(
            block, block, as_s.at[distance, index], as_r.at[distance, index], distance
        )

    def space_attention(index, carry):
        span = block_rows(index)
        bias = []
        for key_block in range(2 * query_blocks):
            kept = mask_ref[frame, half * query_blocks + index, key_block]
            bias.append(jnp.full((1, BLOCK), jnp.where(kept == 1, 0.0, -jnp.inf), jnp.float32))
        bias = jnp.concatenate(bias, axis=1)
        for head in range(local_heads):
            lanes = slice(head * HD, (head + 1) * HD)
            keys = keys_values[:, 0, :, lanes].reshape(2 * rows, HD)
            values = keys_values[:, 1, :, lanes].reshape(2 * rows, HD)
            scores = lax.dot_general(
                queries[span, lanes], keys, NT, preferred_element_type=jnp.float32
            )
            weights = softmax_rounded(scores * scale + bias)
            att_space[me, span, lanes] = jnp.dot(
                weights, values, preferred_element_type=jnp.float32
            ).astype(jnp.bfloat16)
        for distance in range(1, parts):
            att_space_copy(index, distance).start()
        return carry

    lax.fori_loop(0, query_blocks, space_attention, 0)
    load_out(0).wait()
    finish_weights(0)

    def space_project(index, carry):
        span = block_rows(index)
        for distance in range(1, parts):
            att_space_copy(index, distance).wait_recv()
        summed = jnp.zeros((BLOCK, part_width), jnp.float32)
        for part in range(parts):
            summed = summed + jnp.dot(
                att_space[part, span, :], out_weight(0, part), preferred_element_type=jnp.float32
            ).astype(jnp.bfloat16).astype(jnp.float32)
        values = stream[span, :] + mods[0, 2:3] * summed
        stream[span, :] = values
        note_statistics(values, pl.multiple_of(index * BLOCK, BLOCK), BLOCK)
        return carry

    lax.fori_loop(0, query_blocks, space_project, 0)

    send_statistics(1)
    swap_weights(1)
    load_time().wait()
    finish_statistics(1)
    finish_weights(1)

    def time_order(i):
        return lax.rem(frame // per_chunk + 1 + i, chunks)

    def part_copy(index, distance):
        span = chunk_rows(index)
        return fsdp_copy(
            part_sent.at[distance, span], part_got.at[distance, span],
            p_s.at[distance, index], p_r.at[distance, index], distance,
        )

    def kind_lanes(kind):
        return slice(kind * heads_width, (kind + 1) * heads_width)

    def time_send(i, carry):
        index = time_order(i)
        span = chunk_rows(index)
        values = normalised(1, span)
        h_time[span, :] = values
        for distance in range(1, parts):
            for kind in range(3):
                part_sent[distance, span, kind_lanes(kind)] = jnp.dot(
                    values, cross_w[peer(distance), kind], preferred_element_type=jnp.float32
                ).astype(jnp.bfloat16)
            part_copy(index, distance).start()
        return carry

    lax.fori_loop(0, chunks, time_send, 0)

    def time_own(index, carry):
        span = block_rows(index)
        for kind in range(3):
            total[span, kind_lanes(kind)] = jnp.dot(
                h_time[span, :], cross_w[me, kind], preferred_element_type=jnp.float32
            )
        return carry

    lax.fori_loop(0, query_blocks, time_own, 0)
    swap_weights(2)

    def tq_copy(target):
        return seq_copy(
            sent_qkv.at[target], got_qkv.at[frame], tq_s.at[target], tq_r.at[frame],
            target * 2 + half,
        )

    def tq_arrival(origin):
        return seq_copy(
            sent_qkv.at[origin], got_qkv.at[origin], tq_s.at[origin], tq_r.at[origin],
            origin * 2 + half,
        )

    def time_chunk(i, carry):
        index = time_order(i)
        span = chunk_rows(index)
        whole = total[span, :]
        for distance in range(1, parts):
            part_copy(index, distance).wait_recv()
            whole = whole + part_got[distance, span, :].astype(jnp.float32)
        whole = whole.reshape(per_chunk, piece, 3 * heads_width)
        whole = whole.astype(jnp.bfloat16)
        for n in range(per_chunk):
            target = index * per_chunk + n
            sent_qkv[target] = whole[n]

            @pl.when(target != frame)
            def _():
                tq_copy(target).start()

        return carry

    lax.fori_loop(0, chunks, time_chunk, 0)
    got_qkv[frame] = sent_qkv[frame]

    def others(action):
        def step(i, carry):
            action(lax.rem(frame + frames - 1 - i, frames))
            return carry

        lax.fori_loop(0, frames - 1, step, 0)

    others(lambda origin: tq_arrival(origin).wait_recv())

    def position(index):
        passed = jnp.zeros_like(index)
        for n in range(1, frames):
            passed = passed + jnp.where(index >= n * piece, piece, 0)
        return index - passed

    def flat(first):
        return got_qkv[:, :, first:first + HD].astype(jnp.float32).reshape(rows, HD).astype(jnp.bfloat16)

    column = position(lax.broadcasted_iota(jnp.int32, (1, rows), 1))
    for head in range(local_heads):
        first = head * HD
        head_queries = flat(first)
        head_keys = flat(heads_width + first)
        head_values = flat(2 * heads_width + first)
        for block in range(query_blocks):
            span = slice(block * BLOCK, (block + 1) * BLOCK)
            line = position(lax.broadcasted_iota(jnp.int32, (BLOCK, 1), 0) + block * BLOCK)
            scores = lax.dot_general(
                head_queries[span], head_keys, NT, preferred_element_type=jnp.float32
            ) * scale
            weights = softmax_rounded(jnp.where(line == column, scores, -jnp.inf))
            mixed[span, first:first + HD] = jnp.dot(
                weights, head_values, preferred_element_type=jnp.float32
            )
    sent_att[...] = mixed[...].reshape(frames, piece, heads_width).astype(jnp.bfloat16)
    att_time[me, frame] = sent_att[frame]

    def ta_copy(target):
        return seq_copy(
            sent_att.at[target], att_time.at[me, frame], ta_s.at[target], ta_r.at[frame],
            target * 2 + half,
        )

    def ta_arrival(origin):
        return seq_copy(
            sent_att.at[origin], att_time.at[me, origin], ta_s.at[origin], ta_r.at[origin],
            origin * 2 + half,
        )

    def send_att(i, carry):
        ta_copy(lax.rem(frame + 1 + i, frames)).start()
        return carry

    lax.fori_loop(0, frames - 1, send_att, 0)

    def att_time_copy(index, distance):
        block = att_time.at[me, index]
        return fsdp_copy(
            block, block, at_s.at[distance, index], at_r.at[distance, index], distance
        )

    def forward(index):
        for distance in range(1, parts):
            att_time_copy(index, distance).start()

    forward(frame)

    def relay(origin):
        ta_arrival(origin).wait_recv()
        forward(origin)

    others(relay)
    load_out(1).wait()
    finish_weights(2)

    def result_copy(index):
        span = chunk_rows(index)
        return pltpu.make_async_copy(stream.at[span], result_ref.at[0, span], out_sem.at[index])

    def time_project(i, carry):
        index = lax.rem(frame // per_chunk + chunks - i, chunks)
        span = chunk_rows(index)
        for n in range(per_chunk):
            for distance in range(1, parts):
                att_time_copy(index * per_chunk + n, distance).wait_recv()
        summed = jnp.zeros((chunk, part_width), jnp.float32)
        for part in range(parts):
            attended = att_time[part, pl.ds(index * per_chunk, per_chunk)].astype(jnp.float32)
            summed = summed + jnp.dot(
                attended.reshape(chunk, heads_width).astype(jnp.bfloat16), out_weight(1, part),
                preferred_element_type=jnp.float32,
            ).astype(jnp.bfloat16).astype(jnp.float32)
        stream[span, :] = stream[span, :] + mods[1, 2:3] * summed
        result_copy(index).start()
        return carry

    lax.fori_loop(0, chunks, time_project, 0)

    def drain(i, carry):
        kv_copy(i).wait_send()
        for distance in range(1, parts):
            h_copy(i, distance).wait_send()
            part_copy(i, distance).wait_send()
        result_copy(i).wait()
        return carry

    lax.fori_loop(0, chunks, drain, 0)

    def drain_blocks(i, carry):
        for distance in range(1, parts):
            att_space_copy(i, distance).wait_send()
        return carry

    lax.fori_loop(0, query_blocks, drain_blocks, 0)

    def drain_pieces(i, carry):
        for distance in range(1, parts):
            att_time_copy(i, distance).wait_send()
        return carry

    lax.fori_loop(0, frames, drain_pieces, 0)

    def drain_other(target):
        tq_copy(target).wait_send()
        ta_copy(target).wait_send()

    others(drain_other)
    for distance in range(1, parts):
        for layer in range(2):
            stat_copy(layer, distance).wait_send()
        for kind in range(3):
            weight_copy(kind, distance).wait_send()
            core_copy(kind, distance).wait_send()
            ring_steps(lambda step: ring_copy(kind, distance, step, place).wait_send())


def on_device(tokens, block_mask, space_qkv, space_out, space_mod, time_qkv, time_out, time_mod):
    videos, rows, part_width = tokens.shape
    heads_width = space_qkv.shape[2]
    frames = lax.axis_size("seq") // 2
    parts = lax.axis_size("fsdp")
    piece = rows // frames
    chunk = piece if piece % 16 == 0 else 2 * piece
    chunks = rows // chunk
    blocks = rows // BLOCK
    width = part_width * parts
    bf16, f32 = jnp.bfloat16, jnp.float32
    dma = pltpu.SemaphoreType.DMA
    cut_rows = lambda weight: weight.reshape(RING, 2, heads_width // (2 * RING), width)
    hbm = pl.BlockSpec(memory_space=pl.ANY)
    scratch = [
        pltpu.VMEM((rows, part_width), f32),
        pltpu.VMEM((rows, 128), f32),
        pltpu.VMEM((rows, 3 * heads_width), f32),
        pltpu.VMEM((rows, heads_width), bf16),
        pltpu.VMEM((2, 2, rows, heads_width), bf16),
        pltpu.VMEM((rows, heads_width), f32),
        pltpu.VMEM((frames, piece, 3 * heads_width), bf16),
        pltpu.VMEM((frames, piece, 3 * heads_width), bf16),
        pltpu.VMEM((frames, piece, heads_width), bf16),
        pltpu.VMEM((width, 3 * heads_width), bf16),
        pltpu.VMEM((parts, 3, part_width, heads_width), bf16),
        pltpu.VMEM((2, parts, RING, 2, heads_width // (2 * RING), part_width), bf16),
        pltpu.VMEM((2, 3, part_width), f32),
        pltpu.VMEM((2, parts, 8, rows), f32),
        pltpu.VMEM((parts, rows, part_width), bf16),
        pltpu.VMEM((rows, part_width), bf16),
        pltpu.VMEM((parts, rows, 3 * heads_width), bf16),
        pltpu.VMEM((parts, rows, 3 * heads_width), bf16),
        pltpu.VMEM((parts, rows, heads_width), bf16),
        pltpu.VMEM((parts, frames, piece, heads_width), bf16),
        dma, dma((3,)), dma, dma((2,)), dma((2,)), dma((chunks,)),
        dma((2, parts)), dma((2, parts)),
        dma((parts, chunks)), dma((parts, chunks)),
        dma((parts, chunks)), dma((parts, chunks)),
        dma((chunks,)), dma((chunks,)),
        dma((parts, blocks)), dma((parts, blocks)),
        dma((parts, frames)), dma((parts, frames)),
        dma((3, parts)), dma((3, parts)),
        dma((3, parts, RING)), dma((3, parts, RING)),
        dma((3, parts)), dma((3, parts)),
        dma((frames,)), dma((frames,)),
        dma((frames,)), dma((frames,)),
    ]
    sizes = (frames, parts, rows, part_width, heads_width, chunk)
    return pl.pallas_call(
        functools.partial(sublayers, sizes),
        out_shape=jax.ShapeDtypeStruct(tokens.shape, f32),
        in_specs=[pl.BlockSpec(memory_space=pltpu.SMEM)] + [hbm] * 7,
        out_specs=hbm,
        scratch_shapes=scratch,
        compiler_params=pltpu.CompilerParams(
            collective_id=0, has_side_effects=True, vmem_limit_bytes=58 * 1024 * 1024
        ),
        cost_estimate=pl.CostEstimate(
            flops=4 * rows * width * 4 * heads_width, bytes_accessed=20 * 1024 * 1024,
            transcendentals=1024 * 1024,
        ),
    )(
        block_mask, tokens, jnp.swapaxes(space_qkv, 0, 1), cut_rows(space_out), space_mod,
        jnp.swapaxes(time_qkv, 0, 1), cut_rows(time_out), time_mod,
    )


def solution(mesh):
    placed = (
        P(None, "seq", "fsdp"),
        P(),
        P(None, None, "fsdp"),
        P("fsdp", None),
        P(),
        P(None, None, "fsdp"),
        P("fsdp", None),
        P(),
    )
    return jax.shard_map(
        on_device, mesh=mesh, in_specs=placed, out_specs=P(None, "seq", "fsdp"), check_vma=False
    )
```

```python
import functools
import math

import jax
import jax.numpy as jnp
from jax import lax
from jax.experimental import pallas as pl
from jax.experimental.pallas import tpu as pltpu
from jax.sharding import PartitionSpec as P

HD = 128
BLOCK = 128
EPS = 1e-06
RING = 8
STEPS = 4
MESH = pl.DeviceIdType.MESH
NT = (((1,), (1,)), ((), ()))


def softmax_rounded(scores):
    row_max = jnp.max(scores, axis=1, keepdims=True)
    lifted = jnp.exp(scores - row_max)
    return (lifted * (1.0 / jnp.sum(lifted, axis=1, keepdims=True))).astype(jnp.bfloat16)


def sublayers(
    sizes,
    mask_ref, tokens_ref, space_qkv_ref, space_out_ref, space_mod_ref, time_qkv_ref, time_out_ref,
    time_mod_ref, result_ref,
    stream, cols, total, queries, keys_values, mixed, sent_qkv, got_qkv, sent_att,
    space_w, cross_w, out_w, mods, stats, normed, h_time, part_sent, part_got, att_space, att_time,
    in_sem, w_sem, x_sem, o_sem, m_sem, out_sem,
    stat_s, stat_r, h_s, h_r, p_s, p_r, kv_s, kv_r, as_s, as_r, at_s, at_r,
    wq_s, wq_r, wf_s, wf_r, wc_s, wc_r, tq_s, tq_r, ta_s, ta_r,
):
    frames, parts, rows, part_width, heads_width, chunk = sizes
    chunks = rows // chunk
    piece = rows // frames
    per_chunk = chunk // piece
    step_rows = rows // STEPS
    per_step = step_rows // piece
    query_blocks = rows // BLOCK
    local_heads = heads_width // HD
    width = part_width * parts
    slab = part_width // RING
    lane_count = heads_width // 2
    scale = 1.0 / math.sqrt(HD)

    seq = lax.axis_index("seq")
    me = lax.axis_index("fsdp")
    half = lax.rem(seq, 2)
    frame = seq // 2
    place = lax.rem(frame, RING)
    base = frame - place

    def peer(distance):
        return lax.rem(me + distance, parts)

    def source(distance):
        return lax.rem(me + parts - distance, parts)

    def fsdp_copy(src, dst, send, recv, distance):
        return pltpu.make_async_remote_copy(
            src_ref=src, dst_ref=dst, send_sem=send, recv_sem=recv,
            device_id={"fsdp": peer(distance)}, device_id_type=MESH,
        )

    def seq_copy(src, dst, send, recv, target):
        return pltpu.make_async_remote_copy(
            src_ref=src, dst_ref=dst, send_sem=send, recv_sem=recv,
            device_id={"seq": target}, device_id_type=MESH,
        )

    out_refs = (space_out_ref, time_out_ref)
    mod_refs = (space_mod_ref, time_mod_ref)
    own_columns = pl.ds(pl.multiple_of(me * part_width, 128), part_width)
    other_core = seq + 1 - 2 * half

    def load_tokens():
        return pltpu.make_async_copy(tokens_ref.at[0], stream, in_sem)

    def load_space(kind):
        lanes = pl.ds(kind * heads_width, heads_width)
        return pltpu.make_async_copy(
            space_qkv_ref.at[kind], space_w.at[:, lanes], w_sem.at[kind]
        )

    def load_time():
        return pltpu.make_async_copy(
            time_qkv_ref.at[:, own_columns], cross_w.at[me], x_sem
        )

    def load_out(layer):
        return pltpu.make_async_copy(
            out_refs[layer].at[:, :, :, own_columns], out_w.at[layer, me], o_sem.at[layer]
        )

    def load_mod(layer):
        return pltpu.make_async_copy(
            mod_refs[layer].at[:, own_columns], mods.at[layer], m_sem.at[layer]
        )

    load_tokens().start()
    for layer in range(2):
        load_mod(layer).start()
    for kind in range(3):
        load_space(kind).start()

    barrier = pltpu.get_barrier_semaphore()
    for distance in range(1, parts):
        pl.semaphore_signal(barrier, inc=1, device_id={"fsdp": peer(distance)}, device_id_type=MESH)
    for distance in range(1, frames):
        other = lax.rem(frame + distance, frames) * 2 + half
        pl.semaphore_signal(barrier, inc=1, device_id={"seq": other}, device_id_type=MESH)
    pl.semaphore_signal(barrier, inc=1, device_id={"seq": other_core}, device_id_type=MESH)
    pl.semaphore_wait(barrier, parts + frames - 1)

    def slab_rows(first):
        return pl.ds(pl.multiple_of(first, 16), slab)

    own_lanes = pl.ds(pl.multiple_of(half * lane_count, 128), lane_count)

    def weight_piece(kind, owner, index):
        if kind == 1:
            return cross_w.at[owner, :, slab_rows(index * slab), own_lanes]
        return out_w.at[kind // 2, owner, index, half]

    def weight_copy(kind, distance):
        target = peer(distance)
        if kind == 1:
            first = target * part_width + place * slab
            block = time_qkv_ref.at[:, slab_rows(first), own_lanes]
        else:
            columns = pl.ds(pl.multiple_of(target * part_width, 128), part_width)
            block = out_refs[kind // 2].at[place, half, :, columns]
        return fsdp_copy(
            block, weight_piece(kind, me, place),
            wq_s.at[kind, distance], wq_r.at[kind, distance], distance,
        )

    def ring_copy(kind, distance, step, index):
        block = weight_piece(kind, source(distance), index)
        return seq_copy(
            block, block, wf_s.at[kind, distance, step], wf_r.at[kind, distance, step],
            (base + lax.rem(place + step, RING)) * 2 + half,
        )

    def core_copy(kind, distance):
        owner = source(distance)
        if kind == 1:
            block = cross_w.at[owner, :, :, own_lanes]
        else:
            block = out_w.at[kind // 2, owner, :, half]
        return seq_copy(
            block, block, wc_s.at[kind, distance], wc_r.at[kind, distance], other_core
        )

    def ring_steps(action):
        def step(i, carry):
            action(i + 1)
            return carry

        lax.fori_loop(0, RING - 1, step, 0)

    def fetch_weights(kind):
        for distance in range(1, parts):
            weight_copy(kind, distance).start()

    def pass_weights(kind):
        for distance in range(1, parts):
            weight_copy(kind, distance).wait_recv()
            ring_steps(lambda step: ring_copy(kind, distance, step, place).start())

    def swap_weights(kind):
        for distance in range(1, parts):
            ring_steps(
                lambda step: ring_copy(
                    kind, distance, step, lax.rem(place + RING - step, RING)
                ).wait_recv()
            )
            core_copy(kind, distance).start()

    def finish_weights(kind):
        for distance in range(1, parts):
            core_copy(kind, distance).wait_recv()

    def out_weight(layer, part):
        return out_w[layer, part].reshape(heads_width, part_width)

    def note_statistics(values, start, count):
        centre = jnp.sum(values, axis=1, keepdims=True) * (1.0 / part_width)
        offset = values - centre
        spread = jnp.sum(offset * offset, axis=1, keepdims=True)
        lane = lax.broadcasted_iota(jnp.int32, (count, 128), 1)
        cols[pl.ds(start, count), :] = jnp.where(lane == 0, centre, spread)

    def stat_copy(layer, distance):
        return fsdp_copy(
            stats.at[layer, me], stats.at[layer, me],
            stat_s.at[layer, distance], stat_r.at[layer, distance], distance,
        )

    def send_statistics(layer):
        stats[layer, me] = jnp.transpose(cols[...])[:8]
        for distance in range(1, parts):
            stat_copy(layer, distance).start()

    def finish_statistics(layer):
        for distance in range(1, parts):
            stat_copy(layer, distance).wait_recv()
        centre = jnp.zeros((1, rows), jnp.float32)
        for part in range(parts):
            centre = centre + stats[layer, part][0:1]
        centre = centre * (1.0 / parts)
        spread = jnp.zeros((1, rows), jnp.float32)
        for part in range(parts):
            shift = stats[layer, part][0:1] - centre
            spread = spread + stats[layer, part][1:2] * (1.0 / part_width) + shift * shift
        inverse = lax.rsqrt(spread * (1.0 / parts) + EPS)
        line = lax.broadcasted_iota(jnp.int32, (128, rows), 0)
        cols[...] = jnp.transpose(jnp.where(line == 0, centre, inverse))

    def chunk_rows(index):
        return pl.ds(pl.multiple_of(index * chunk, chunk), chunk)

    def block_rows(index):
        return pl.ds(pl.multiple_of(index * BLOCK, BLOCK), BLOCK)

    def h_copy(index, distance):
        block = normed.at[me, chunk_rows(index)]
        return fsdp_copy(
            block, block, h_s.at[distance, index], h_r.at[distance, index], distance
        )

    def normalised(layer, span):
        line = cols[span, :]
        shift = mods[layer, 0:1]
        gain = 1.0 + mods[layer, 1:2]
        values = (stream[span, :] - line[:, 0:1]) * line[:, 1:2] * gain + shift
        return values.astype(jnp.bfloat16)

    load_tokens().wait()

    def first_statistics(i, carry):
        start = pl.multiple_of(i * chunk, chunk)
        note_statistics(stream[pl.ds(start, chunk), :], start, chunk)
        return carry

    lax.fori_loop(0, chunks, first_statistics, 0)
    send_statistics(0)
    for kind in range(3):
        fetch_weights(kind)
    for layer in range(2):
        load_mod(layer).wait()
    load_time().start()
    load_out(0).start()
    load_out(1).start()
    finish_statistics(0)

    def space_send(index, carry):
        span = chunk_rows(index)
        normed[me, span, :] = normalised(0, span)
        for distance in range(1, parts):
            h_copy(index, distance).start()
        return carry

    lax.fori_loop(0, chunks, space_send, 0)
    for kind in range(3):
        pass_weights(kind)
    for kind in range(3):
        load_space(kind).wait()

    def space_depth(owner):
        return pl.ds(pl.multiple_of(owner * part_width, 128), part_width)

    def space_own(index, carry):
        span = block_rows(index)
        total[span, :] = jnp.dot(
            normed[me, span, :], space_w[space_depth(me), :], preferred_element_type=jnp.float32
        )
        return carry

    lax.fori_loop(0, query_blocks, space_own, 0)

    def kv_copy(index):
        block = keys_values.at[half, :, chunk_rows(index)]
        return seq_copy(block, block, kv_s.at[index], kv_r.at[index], other_core)

    def space_chunk(index, carry):
        span = chunk_rows(index)
        value = total[span, :]
        for distance in range(1, parts):
            h_copy(index, distance).wait_recv()
            other = source(distance)
            value = value + jnp.dot(
                normed[other, span, :], space_w[space_depth(other), :],
                preferred_element_type=jnp.float32,
            )
        value = value.astype(jnp.bfloat16)
        queries[span, :] = value[:, :heads_width]
        for kind in range(2):
            first = (kind + 1) * heads_width
            keys_values[half, kind, span, :] = value[:, first:first + heads_width]
        kv_copy(index).start()
        return carry

    lax.fori_loop(0, chunks, space_chunk, 0)
    swap_weights(0)

    def wait_keys(index, carry):
        kv_copy(index).wait_recv()
        return carry

    lax.fori_loop(0, chunks, wait_keys, 0)

    def att_space_copy(index, distance):
        block = att_space.at[me, block_rows(index)]
        return fsdp_copy(
            block, block, as_s.at[distance, index], as_r.at[distance, index], distance
        )

    def space_attention(index, carry):
        span = block_rows(index)
        bias = []
        for key_block in range(2 * query_blocks):
            kept = mask_ref[half * query_blocks + index, frame, key_block]
            bias.append(jnp.full((1, BLOCK), jnp.where(kept == 1, 0.0, -jnp.inf), jnp.float32))
        bias = jnp.concatenate(bias, axis=1)
        for head in range(local_heads):
            lanes = slice(head * HD, (head + 1) * HD)
            keys = keys_values[:, 0, :, lanes].reshape(2 * rows, HD)
            values = keys_values[:, 1, :, lanes].reshape(2 * rows, HD)
            scores = lax.dot_general(
                queries[span, lanes], keys, NT, preferred_element_type=jnp.float32
            )
            weights = softmax_rounded(scores * scale + bias)
            att_space[me, span, lanes] = jnp.dot(
                weights, values, preferred_element_type=jnp.float32
            ).astype(jnp.bfloat16)
        for distance in range(1, parts):
            att_space_copy(index, distance).start()
        return carry

    lax.fori_loop(0, query_blocks, space_attention, 0)
    load_out(0).wait()
    finish_weights(0)

    def space_project(index, carry):
        span = block_rows(index)
        for distance in range(1, parts):
            att_space_copy(index, distance).wait_recv()
        summed = jnp.zeros((BLOCK, part_width), jnp.float32)
        for part in range(parts):
            summed = summed + jnp.dot(
                att_space[part, span, :], out_weight(0, part), preferred_element_type=jnp.float32
            ).astype(jnp.bfloat16).astype(jnp.float32)
        values = stream[span, :] + mods[0, 2:3] * summed
        stream[span, :] = values
        note_statistics(values, pl.multiple_of(index * BLOCK, BLOCK), BLOCK)
        return carry

    lax.fori_loop(0, query_blocks, space_project, 0)

    send_statistics(1)
    swap_weights(1)
    load_time().wait()
    finish_statistics(1)
    finish_weights(1)

    def time_order(i):
        return lax.rem(frame // per_step + 1 + i, STEPS)

    def step_span(index):
        return pl.ds(pl.multiple_of(index * step_rows, step_rows), step_rows)

    def part_copy(index, distance):
        span = step_span(index)
        return fsdp_copy(
            part_sent.at[distance, span], part_got.at[distance, span],
            p_s.at[distance, index], p_r.at[distance, index], distance,
        )

    def kind_lanes(kind):
        return slice(kind * heads_width, (kind + 1) * heads_width)

    def time_send(i):
        index = time_order(i)
        span = step_span(index)
        values = normalised(1, span)
        h_time[span, :] = values
        for distance in range(1, parts):
            for kind in range(3):
                part_sent[distance, span, kind_lanes(kind)] = jnp.dot(
                    values, cross_w[peer(distance), kind], preferred_element_type=jnp.float32
                ).astype(jnp.bfloat16)
            part_copy(index, distance).start()
        for kind in range(3):
            total[span, kind_lanes(kind)] = jnp.dot(
                h_time[span, :], cross_w[me, kind], preferred_element_type=jnp.float32
            )

    def tq_copy(target):
        return seq_copy(
            sent_qkv.at[target], got_qkv.at[frame], tq_s.at[target], tq_r.at[frame],
            target * 2 + half,
        )

    def tq_arrival(origin):
        return seq_copy(
            sent_qkv.at[origin], got_qkv.at[origin], tq_s.at[origin], tq_r.at[origin],
            origin * 2 + half,
        )

    def time_pass(i):
        index = time_order(i)
        span = step_span(index)
        whole = total[span, :]
        for distance in range(1, parts):
            part_copy(index, distance).wait_recv()
            whole = whole + part_got[distance, span, :].astype(jnp.float32)
        whole = whole.reshape(per_step, piece, 3 * heads_width).astype(jnp.bfloat16)
        for n in range(per_step):
            target = index * per_step + n
            sent_qkv[target] = whole[n]

            @pl.when(target != frame)
            def _():
                tq_copy(target).start()

    time_send(0)

    def time_step(i, carry):
        time_send(i)
        time_pass(i - 1)
        return carry

    lax.fori_loop(1, STEPS, time_step, 0)
    time_pass(STEPS - 1)
    swap_weights(2)
    got_qkv[frame] = sent_qkv[frame]

    def others(action):
        def step(i, carry):
            action(lax.rem(frame + frames - 1 - i, frames))
            return carry

        lax.fori_loop(0, frames - 1, step, 0)

    others(lambda origin: tq_arrival(origin).wait_recv())

    def position(index):
        passed = jnp.zeros_like(index)
        for n in range(1, frames):
            passed = passed + jnp.where(index >= n * piece, piece, 0)
        return index - passed

    def flat(first):
        return got_qkv[:, :, first:first + HD].astype(jnp.float32).reshape(rows, HD).astype(jnp.bfloat16)

    column = position(lax.broadcasted_iota(jnp.int32, (1, rows), 1))
    for head in range(local_heads):
        first = head * HD
        head_queries = flat(first)
        head_keys = flat(heads_width + first)
        head_values = flat(2 * heads_width + first)
        for block in range(query_blocks):
            span = slice(block * BLOCK, (block + 1) * BLOCK)
            line = position(lax.broadcasted_iota(jnp.int32, (BLOCK, 1), 0) + block * BLOCK)
            scores = lax.dot_general(
                head_queries[span], head_keys, NT, preferred_element_type=jnp.float32
            ) * scale
            weights = softmax_rounded(jnp.where(line == column, scores, -jnp.inf))
            mixed[span, first:first + HD] = jnp.dot(
                weights, head_values, preferred_element_type=jnp.float32
            )
    sent_att[...] = mixed[...].reshape(frames, piece, heads_width).astype(jnp.bfloat16)
    att_time[me, frame] = sent_att[frame]

    def ta_copy(target):
        return seq_copy(
            sent_att.at[target], att_time.at[me, frame], ta_s.at[target], ta_r.at[frame],
            target * 2 + half,
        )

    def ta_arrival(origin):
        return seq_copy(
            sent_att.at[origin], att_time.at[me, origin], ta_s.at[origin], ta_r.at[origin],
            origin * 2 + half,
        )

    def send_att(i, carry):
        ta_copy(lax.rem(frame + 1 + i, frames)).start()
        return carry

    lax.fori_loop(0, frames - 1, send_att, 0)

    def att_time_copy(index, distance):
        block = att_time.at[me, index]
        return fsdp_copy(
            block, block, at_s.at[distance, index], at_r.at[distance, index], distance
        )

    def forward(index):
        for distance in range(1, parts):
            att_time_copy(index, distance).start()

    forward(frame)

    def relay(origin):
        ta_arrival(origin).wait_recv()
        forward(origin)

    others(relay)
    load_out(1).wait()
    finish_weights(2)

    def result_copy(index):
        span = chunk_rows(index)
        return pltpu.make_async_copy(stream.at[span], result_ref.at[0, span], out_sem.at[index])

    def time_project(i, carry):
        index = lax.rem(frame // per_chunk + chunks - i, chunks)
        span = chunk_rows(index)
        for n in range(per_chunk):
            for distance in range(1, parts):
                att_time_copy(index * per_chunk + n, distance).wait_recv()
        summed = jnp.zeros((chunk, part_width), jnp.float32)
        for part in range(parts):
            attended = att_time[part, pl.ds(index * per_chunk, per_chunk)].astype(jnp.float32)
            summed = summed + jnp.dot(
                attended.reshape(chunk, heads_width).astype(jnp.bfloat16), out_weight(1, part),
                preferred_element_type=jnp.float32,
            ).astype(jnp.bfloat16).astype(jnp.float32)
        stream[span, :] = stream[span, :] + mods[1, 2:3] * summed
        result_copy(index).start()
        return carry

    lax.fori_loop(0, chunks, time_project, 0)

    def drain(i, carry):
        kv_copy(i).wait_send()
        for distance in range(1, parts):
            h_copy(i, distance).wait_send()
        result_copy(i).wait()
        return carry

    lax.fori_loop(0, chunks, drain, 0)

    def drain_steps(i, carry):
        for distance in range(1, parts):
            part_copy(i, distance).wait_send()
        return carry

    lax.fori_loop(0, STEPS, drain_steps, 0)

    def drain_blocks(i, carry):
        for distance in range(1, parts):
            att_space_copy(i, distance).wait_send()
        return carry

    lax.fori_loop(0, query_blocks, drain_blocks, 0)

    def drain_pieces(i, carry):
        for distance in range(1, parts):
            att_time_copy(i, distance).wait_send()
        return carry

    lax.fori_loop(0, frames, drain_pieces, 0)

    def drain_other(target):
        tq_copy(target).wait_send()
        ta_copy(target).wait_send()

    others(drain_other)
    for distance in range(1, parts):
        for layer in range(2):
            stat_copy(layer, distance).wait_send()
        for kind in range(3):
            weight_copy(kind, distance).wait_send()
            core_copy(kind, distance).wait_send()
            ring_steps(lambda step: ring_copy(kind, distance, step, place).wait_send())


def on_device(tokens, block_mask, space_qkv, space_out, space_mod, time_qkv, time_out, time_mod):
    videos, rows, part_width = tokens.shape
    heads_width = space_qkv.shape[2]
    frames = lax.axis_size("seq") // 2
    parts = lax.axis_size("fsdp")
    piece = rows // frames
    chunk = piece if piece % 16 == 0 else 2 * piece
    chunks = rows // chunk
    blocks = rows // BLOCK
    width = part_width * parts
    bf16, f32 = jnp.bfloat16, jnp.float32
    dma = pltpu.SemaphoreType.DMA
    cut_rows = lambda weight: weight.reshape(RING, 2, heads_width // (2 * RING), width)
    hbm = pl.BlockSpec(memory_space=pl.ANY)
    scratch = [
        pltpu.VMEM((rows, part_width), f32),
        pltpu.VMEM((rows, 128), f32),
        pltpu.VMEM((rows, 3 * heads_width), f32),
        pltpu.VMEM((rows, heads_width), bf16),
        pltpu.VMEM((2, 2, rows, heads_width), bf16),
        pltpu.VMEM((rows, heads_width), f32),
        pltpu.VMEM((frames, piece, 3 * heads_width), bf16),
        pltpu.VMEM((frames, piece, 3 * heads_width), bf16),
        pltpu.VMEM((frames, piece, heads_width), bf16),
        pltpu.VMEM((width, 3 * heads_width), bf16),
        pltpu.VMEM((parts, 3, part_width, heads_width), bf16),
        pltpu.VMEM((2, parts, RING, 2, heads_width // (2 * RING), part_width), bf16),
        pltpu.VMEM((2, 3, part_width), f32),
        pltpu.VMEM((2, parts, 8, rows), f32),
        pltpu.VMEM((parts, rows, part_width), bf16),
        pltpu.VMEM((rows, part_width), bf16),
        pltpu.VMEM((parts, rows, 3 * heads_width), bf16),
        pltpu.VMEM((parts, rows, 3 * heads_width), bf16),
        pltpu.VMEM((parts, rows, heads_width), bf16),
        pltpu.VMEM((parts, frames, piece, heads_width), bf16),
        dma, dma((3,)), dma, dma((2,)), dma((2,)), dma((chunks,)),
        dma((2, parts)), dma((2, parts)),
        dma((parts, chunks)), dma((parts, chunks)),
        dma((parts, STEPS)), dma((parts, STEPS)),
        dma((chunks,)), dma((chunks,)),
        dma((parts, blocks)), dma((parts, blocks)),
        dma((parts, frames)), dma((parts, frames)),
        dma((3, parts)), dma((3, parts)),
        dma((3, parts, RING)), dma((3, parts, RING)),
        dma((3, parts)), dma((3, parts)),
        dma((frames,)), dma((frames,)),
        dma((frames,)), dma((frames,)),
    ]
    sizes = (frames, parts, rows, part_width, heads_width, chunk)
    return pl.pallas_call(
        functools.partial(sublayers, sizes),
        out_shape=jax.ShapeDtypeStruct(tokens.shape, f32),
        in_specs=[pl.BlockSpec(memory_space=pltpu.SMEM)] + [hbm] * 7,
        out_specs=hbm,
        scratch_shapes=scratch,
        compiler_params=pltpu.CompilerParams(
            collective_id=0, has_side_effects=True, vmem_limit_bytes=58 * 1024 * 1024
        ),
        cost_estimate=pl.CostEstimate(
            flops=4 * rows * width * 4 * heads_width, bytes_accessed=20 * 1024 * 1024,
            transcendentals=1024 * 1024,
        ),
    )(
        jnp.swapaxes(block_mask, 0, 1), tokens, jnp.swapaxes(space_qkv, 0, 1), cut_rows(space_out), space_mod,
        jnp.swapaxes(time_qkv, 0, 1), cut_rows(time_out), time_mod,
    )


def solution(mesh):
    placed = (
        P(None, "seq", "fsdp"),
        P(),
        P(None, None, "fsdp"),
        P("fsdp", None),
        P(),
        P(None, None, "fsdp"),
        P("fsdp", None),
        P(),
    )
    return jax.shard_map(
        on_device, mesh=mesh, in_specs=placed, out_specs=P(None, "seq", "fsdp"), check_vma=False
    )
```

```python
import functools
import math

import jax
import jax.numpy as jnp
from jax import lax
from jax.experimental import pallas as pl
from jax.experimental.pallas import tpu as pltpu
from jax.sharding import PartitionSpec as P

HD = 128
BLOCK = 128
EPS = 1e-06
RING = 8
STEPS = 4
MESH = pl.DeviceIdType.MESH
NT = (((1,), (1,)), ((), ()))


def softmax_rounded(scores):
    row_max = jnp.max(scores, axis=1, keepdims=True)
    lifted = jnp.exp(scores - row_max)
    return (lifted * (1.0 / jnp.sum(lifted, axis=1, keepdims=True))).astype(jnp.bfloat16)


def sublayers(
    sizes,
    mask_ref, tokens_ref, space_qkv_ref, space_out_ref, space_mod_ref, time_qkv_ref, time_out_ref,
    time_mod_ref, result_ref,
    stream, cols, total, queries, keys_values, mixed, sent_qkv, got_qkv, sent_att,
    space_w, cross_w, out_w, mods, stats, normed, h_time, part_sent, part_got, att_space, att_time,
    in_sem, w_sem, x_sem, o_sem, m_sem, out_sem,
    stat_s, stat_r, h_s, h_r, p_s, p_r, kv_s, kv_r, as_s, as_r, at_s, at_r,
    wq_s, wq_r, wf_s, wf_r, wc_s, wc_r, tq_s, tq_r, ta_s, ta_r,
):
    frames, parts, rows, part_width, heads_width, chunk = sizes
    chunks = rows // chunk
    piece = rows // frames
    per_chunk = chunk // piece
    step_rows = rows // STEPS
    per_step = step_rows // piece
    query_blocks = rows // BLOCK
    local_heads = heads_width // HD
    width = part_width * parts
    slab = part_width // RING
    lane_count = heads_width // 2
    scale = 1.0 / math.sqrt(HD)

    seq = lax.axis_index("seq")
    me = lax.axis_index("fsdp")
    half = lax.rem(seq, 2)
    frame = seq // 2
    place = lax.rem(frame, RING)
    base = frame - place

    def peer(distance):
        return lax.rem(me + distance, parts)

    def source(distance):
        return lax.rem(me + parts - distance, parts)

    def fsdp_copy(src, dst, send, recv, distance):
        return pltpu.make_async_remote_copy(
            src_ref=src, dst_ref=dst, send_sem=send, recv_sem=recv,
            device_id={"fsdp": peer(distance)}, device_id_type=MESH,
        )

    def seq_copy(src, dst, send, recv, target):
        return pltpu.make_async_remote_copy(
            src_ref=src, dst_ref=dst, send_sem=send, recv_sem=recv,
            device_id={"seq": target}, device_id_type=MESH,
        )

    out_refs = (space_out_ref, time_out_ref)
    mod_refs = (space_mod_ref, time_mod_ref)
    own_columns = pl.ds(pl.multiple_of(me * part_width, 128), part_width)
    other_core = seq + 1 - 2 * half

    def load_tokens():
        return pltpu.make_async_copy(tokens_ref.at[0], stream, in_sem)

    def load_space(kind):
        lanes = pl.ds(kind * heads_width, heads_width)
        return pltpu.make_async_copy(
            space_qkv_ref.at[kind], space_w.at[:, lanes], w_sem.at[kind]
        )

    def load_time():
        return pltpu.make_async_copy(
            time_qkv_ref.at[:, own_columns], cross_w.at[me], x_sem
        )

    def load_out(layer):
        return pltpu.make_async_copy(
            out_refs[layer].at[:, :, :, own_columns], out_w.at[layer, me], o_sem.at[layer]
        )

    def load_mod(layer):
        return pltpu.make_async_copy(
            mod_refs[layer].at[:, own_columns], mods.at[layer], m_sem.at[layer]
        )

    load_tokens().start()
    for layer in range(2):
        load_mod(layer).start()
    for kind in range(3):
        load_space(kind).start()

    barrier = pltpu.get_barrier_semaphore()
    for distance in range(1, parts):
        pl.semaphore_signal(barrier, inc=1, device_id={"fsdp": peer(distance)}, device_id_type=MESH)
    for distance in range(1, frames):
        other = lax.rem(frame + distance, frames) * 2 + half
        pl.semaphore_signal(barrier, inc=1, device_id={"seq": other}, device_id_type=MESH)
    pl.semaphore_signal(barrier, inc=1, device_id={"seq": other_core}, device_id_type=MESH)
    pl.semaphore_wait(barrier, parts + frames - 1)

    def slab_rows(first):
        return pl.ds(pl.multiple_of(first, 16), slab)

    own_lanes = pl.ds(pl.multiple_of(half * lane_count, 128), lane_count)

    def weight_piece(kind, owner, index):
        if kind == 1:
            return cross_w.at[owner, :, slab_rows(index * slab), own_lanes]
        return out_w.at[kind // 2, owner, index, half]

    def weight_copy(kind, distance):
        target = peer(distance)
        if kind == 1:
            first = target * part_width + place * slab
            block = time_qkv_ref.at[:, slab_rows(first), own_lanes]
        else:
            columns = pl.ds(pl.multiple_of(target * part_width, 128), part_width)
            block = out_refs[kind // 2].at[place, half, :, columns]
        return fsdp_copy(
            block, weight_piece(kind, me, place),
            wq_s.at[kind, distance], wq_r.at[kind, distance], distance,
        )

    twin = place + 1 - 2 * lax.rem(place, 2)
    half_ring = RING // 2

    def place_copy(kind, distance, slot, index, target):
        block = weight_piece(kind, source(distance), index)
        return seq_copy(
            block, block, wf_s.at[kind, distance, slot], wf_r.at[kind, distance, slot],
            (base + target) * 2 + half,
        )

    def ring_copy(kind, distance, step, index):
        return place_copy(kind, distance, step, index, lax.rem(place + 2 * step, RING))

    def twin_copy(kind, distance, step, own):
        index = lax.rem(own + RING - 2 * step, RING)
        return place_copy(kind, distance, half_ring + step, index, twin)

    def core_copy(kind, distance):
        owner = source(distance)
        if kind == 1:
            block = cross_w.at[owner, :, :, own_lanes]
        else:
            block = out_w.at[kind // 2, owner, :, half]
        return seq_copy(
            block, block, wc_s.at[kind, distance], wc_r.at[kind, distance], other_core
        )

    def fetch_weights(kind):
        for distance in range(1, parts):
            weight_copy(kind, distance).start()

    def pass_weights(kind):
        for distance in range(1, parts):
            weight_copy(kind, distance).wait_recv()
            for step in range(1, half_ring):
                ring_copy(kind, distance, step, place).start()
            twin_copy(kind, distance, 0, place).start()

    def relay_weights(kind):
        for distance in range(1, parts):
            for step in range(1, half_ring):
                ring_copy(kind, distance, step, lax.rem(place + RING - 2 * step, RING)).wait_recv()
                twin_copy(kind, distance, step, place).start()

    def swap_weights(kind):
        for distance in range(1, parts):
            for step in range(half_ring):
                twin_copy(kind, distance, step, twin).wait_recv()
            core_copy(kind, distance).start()

    def finish_weights(kind):
        for distance in range(1, parts):
            core_copy(kind, distance).wait_recv()

    def out_weight(layer, part):
        return out_w[layer, part].reshape(heads_width, part_width)

    def note_statistics(values, start, count):
        centre = jnp.sum(values, axis=1, keepdims=True) * (1.0 / part_width)
        offset = values - centre
        spread = jnp.sum(offset * offset, axis=1, keepdims=True)
        lane = lax.broadcasted_iota(jnp.int32, (count, 128), 1)
        cols[pl.ds(start, count), :] = jnp.where(lane == 0, centre, spread)

    def stat_copy(layer, distance):
        return fsdp_copy(
            stats.at[layer, me], stats.at[layer, me],
            stat_s.at[layer, distance], stat_r.at[layer, distance], distance,
        )

    def send_statistics(layer):
        stats[layer, me] = jnp.transpose(cols[...])[:8]
        for distance in range(1, parts):
            stat_copy(layer, distance).start()

    def finish_statistics(layer):
        for distance in range(1, parts):
            stat_copy(layer, distance).wait_recv()
        centre = jnp.zeros((1, rows), jnp.float32)
        for part in range(parts):
            centre = centre + stats[layer, part][0:1]
        centre = centre * (1.0 / parts)
        spread = jnp.zeros((1, rows), jnp.float32)
        for part in range(parts):
            shift = stats[layer, part][0:1] - centre
            spread = spread + stats[layer, part][1:2] * (1.0 / part_width) + shift * shift
        inverse = lax.rsqrt(spread * (1.0 / parts) + EPS)
        line = lax.broadcasted_iota(jnp.int32, (128, rows), 0)
        cols[...] = jnp.transpose(jnp.where(line == 0, centre, inverse))

    def chunk_rows(index):
        return pl.ds(pl.multiple_of(index * chunk, chunk), chunk)

    def block_rows(index):
        return pl.ds(pl.multiple_of(index * BLOCK, BLOCK), BLOCK)

    def h_copy(index, distance):
        block = normed.at[me, chunk_rows(index)]
        return fsdp_copy(
            block, block, h_s.at[distance, index], h_r.at[distance, index], distance
        )

    def normalised(layer, span):
        line = cols[span, :]
        shift = mods[layer, 0:1]
        gain = 1.0 + mods[layer, 1:2]
        values = (stream[span, :] - line[:, 0:1]) * line[:, 1:2] * gain + shift
        return values.astype(jnp.bfloat16)

    load_tokens().wait()

    def first_statistics(i, carry):
        start = pl.multiple_of(i * chunk, chunk)
        note_statistics(stream[pl.ds(start, chunk), :], start, chunk)
        return carry

    lax.fori_loop(0, chunks, first_statistics, 0)
    send_statistics(0)
    for kind in range(3):
        fetch_weights(kind)
    for layer in range(2):
        load_mod(layer).wait()
    load_time().start()
    load_out(0).start()
    load_out(1).start()
    finish_statistics(0)

    def space_send(index, carry):
        span = chunk_rows(index)
        normed[me, span, :] = normalised(0, span)
        for distance in range(1, parts):
            h_copy(index, distance).start()
        return carry

    lax.fori_loop(0, chunks, space_send, 0)
    for kind in range(3):
        pass_weights(kind)
    for kind in range(3):
        load_space(kind).wait()

    def space_depth(owner):
        return pl.ds(pl.multiple_of(owner * part_width, 128), part_width)

    def space_own(index, carry):
        span = block_rows(index)
        total[span, :] = jnp.dot(
            normed[me, span, :], space_w[space_depth(me), :], preferred_element_type=jnp.float32
        )
        return carry

    lax.fori_loop(0, query_blocks, space_own, 0)

    def kv_copy(index):
        block = keys_values.at[half, :, chunk_rows(index)]
        return seq_copy(block, block, kv_s.at[index], kv_r.at[index], other_core)

    def space_chunk(index, carry):
        span = chunk_rows(index)
        value = total[span, :]
        for distance in range(1, parts):
            h_copy(index, distance).wait_recv()
            other = source(distance)
            value = value + jnp.dot(
                normed[other, span, :], space_w[space_depth(other), :],
                preferred_element_type=jnp.float32,
            )
        value = value.astype(jnp.bfloat16)
        queries[span, :] = value[:, :heads_width]
        for kind in range(2):
            first = (kind + 1) * heads_width
            keys_values[half, kind, span, :] = value[:, first:first + heads_width]
        kv_copy(index).start()
        return carry

    relay_weights(0)
    lax.fori_loop(0, chunks // 2, space_chunk, 0)
    relay_weights(1)
    lax.fori_loop(chunks // 2, chunks, space_chunk, 0)
    relay_weights(2)
    swap_weights(0)

    def wait_keys(index, carry):
        kv_copy(index).wait_recv()
        return carry

    lax.fori_loop(0, chunks, wait_keys, 0)

    def att_space_copy(index, distance):
        block = att_space.at[me, block_rows(index)]
        return fsdp_copy(
            block, block, as_s.at[distance, index], as_r.at[distance, index], distance
        )

    def space_attention(index, carry):
        span = block_rows(index)
        bias = []
        for key_block in range(2 * query_blocks):
            kept = mask_ref[half * query_blocks + index, frame, key_block]
            bias.append(jnp.full((1, BLOCK), jnp.where(kept == 1, 0.0, -jnp.inf), jnp.float32))
        bias = jnp.concatenate(bias, axis=1)
        for head in range(local_heads):
            lanes = slice(head * HD, (head + 1) * HD)
            keys = keys_values[:, 0, :, lanes].reshape(2 * rows, HD)
            values = keys_values[:, 1, :, lanes].reshape(2 * rows, HD)
            scores = lax.dot_general(
                queries[span, lanes], keys, NT, preferred_element_type=jnp.float32
            )
            weights = softmax_rounded(scores * scale + bias)
            att_space[me, span, lanes] = jnp.dot(
                weights, values, preferred_element_type=jnp.float32
            ).astype(jnp.bfloat16)
        for distance in range(1, parts):
            att_space_copy(index, distance).start()
        return carry

    lax.fori_loop(0, query_blocks, space_attention, 0)
    load_out(0).wait()
    finish_weights(0)

    def space_project(index, carry):
        span = block_rows(index)
        for distance in range(1, parts):
            att_space_copy(index, distance).wait_recv()
        summed = jnp.zeros((BLOCK, part_width), jnp.float32)
        for part in range(parts):
            summed = summed + jnp.dot(
                att_space[part, span, :], out_weight(0, part), preferred_element_type=jnp.float32
            ).astype(jnp.bfloat16).astype(jnp.float32)
        values = stream[span, :] + mods[0, 2:3] * summed
        stream[span, :] = values
        note_statistics(values, pl.multiple_of(index * BLOCK, BLOCK), BLOCK)
        return carry

    lax.fori_loop(0, query_blocks, space_project, 0)

    send_statistics(1)
    swap_weights(1)
    load_time().wait()
    finish_statistics(1)
    finish_weights(1)

    def time_order(i):
        return lax.rem(frame // per_step + 1 + i, STEPS)

    def step_span(index):
        return pl.ds(pl.multiple_of(index * step_rows, step_rows), step_rows)

    def part_copy(index, distance):
        span = step_span(index)
        return fsdp_copy(
            part_sent.at[distance, span], part_got.at[distance, span],
            p_s.at[distance, index], p_r.at[distance, index], distance,
        )

    def kind_lanes(kind):
        return slice(kind * heads_width, (kind + 1) * heads_width)

    def time_send(i):
        index = time_order(i)
        span = step_span(index)
        values = normalised(1, span)
        h_time[span, :] = values
        for distance in range(1, parts):
            for kind in range(3):
                part_sent[distance, span, kind_lanes(kind)] = jnp.dot(
                    values, cross_w[peer(distance), kind], preferred_element_type=jnp.float32
                ).astype(jnp.bfloat16)
            part_copy(index, distance).start()
        for kind in range(3):
            total[span, kind_lanes(kind)] = jnp.dot(
                h_time[span, :], cross_w[me, kind], preferred_element_type=jnp.float32
            )

    def tq_copy(target):
        return seq_copy(
            sent_qkv.at[target], got_qkv.at[frame], tq_s.at[target], tq_r.at[frame],
            target * 2 + half,
        )

    def tq_arrival(origin):
        return seq_copy(
            sent_qkv.at[origin], got_qkv.at[origin], tq_s.at[origin], tq_r.at[origin],
            origin * 2 + half,
        )

    def time_pass(i):
        index = time_order(i)
        span = step_span(index)
        whole = total[span, :]
        for distance in range(1, parts):
            part_copy(index, distance).wait_recv()
            whole = whole + part_got[distance, span, :].astype(jnp.float32)
        whole = whole.reshape(per_step, piece, 3 * heads_width).astype(jnp.bfloat16)
        for n in range(per_step):
            target = index * per_step + n
            sent_qkv[target] = whole[n]

            @pl.when(target != frame)
            def _():
                tq_copy(target).start()

    time_send(0)

    def time_step(i, carry):
        time_send(i)
        time_pass(i - 1)
        return carry

    lax.fori_loop(1, STEPS, time_step, 0)
    time_pass(STEPS - 1)
    got_qkv[frame] = sent_qkv[frame]

    def others(action):
        def step(i, carry):
            action(lax.rem(frame + frames - 1 - i, frames))
            return carry

        lax.fori_loop(0, frames - 1, step, 0)

    others(lambda origin: tq_arrival(origin).wait_recv())

    def position(index):
        passed = jnp.zeros_like(index)
        for n in range(1, frames):
            passed = passed + jnp.where(index >= n * piece, piece, 0)
        return index - passed

    def flat(first):
        return got_qkv[:, :, first:first + HD].astype(jnp.float32).reshape(rows, HD).astype(jnp.bfloat16)

    column = position(lax.broadcasted_iota(jnp.int32, (1, rows), 1))
    for head in range(local_heads):
        first = head * HD
        head_queries = flat(first)
        head_keys = flat(heads_width + first)
        head_values = flat(2 * heads_width + first)
        for block in range(query_blocks):
            span = slice(block * BLOCK, (block + 1) * BLOCK)
            line = position(lax.broadcasted_iota(jnp.int32, (BLOCK, 1), 0) + block * BLOCK)
            scores = lax.dot_general(
                head_queries[span], head_keys, NT, preferred_element_type=jnp.float32
            ) * scale
            weights = softmax_rounded(jnp.where(line == column, scores, -jnp.inf))
            mixed[span, first:first + HD] = jnp.dot(
                weights, head_values, preferred_element_type=jnp.float32
            )
    sent_att[...] = mixed[...].reshape(frames, piece, heads_width).astype(jnp.bfloat16)
    att_time[me, frame] = sent_att[frame]

    def ta_copy(target):
        return seq_copy(
            sent_att.at[target], att_time.at[me, frame], ta_s.at[target], ta_r.at[frame],
            target * 2 + half,
        )

    def ta_arrival(origin):
        return seq_copy(
            sent_att.at[origin], att_time.at[me, origin], ta_s.at[origin], ta_r.at[origin],
            origin * 2 + half,
        )

    def send_att(i, carry):
        ta_copy(lax.rem(frame + 1 + i, frames)).start()
        return carry

    lax.fori_loop(0, frames - 1, send_att, 0)

    def att_time_copy(index, distance):
        block = att_time.at[me, index]
        return fsdp_copy(
            block, block, at_s.at[distance, index], at_r.at[distance, index], distance
        )

    def forward(index):
        for distance in range(1, parts):
            att_time_copy(index, distance).start()

    forward(frame)
    swap_weights(2)

    def relay(origin):
        ta_arrival(origin).wait_recv()
        forward(origin)

    others(relay)
    load_out(1).wait()
    finish_weights(2)

    def result_copy(index):
        span = chunk_rows(index)
        return pltpu.make_async_copy(stream.at[span], result_ref.at[0, span], out_sem.at[index])

    def time_project(i, carry):
        index = lax.rem(frame // per_chunk + chunks - i, chunks)
        span = chunk_rows(index)
        for n in range(per_chunk):
            for distance in range(1, parts):
                att_time_copy(index * per_chunk + n, distance).wait_recv()
        summed = jnp.zeros((chunk, part_width), jnp.float32)
        for part in range(parts):
            attended = att_time[part, pl.ds(index * per_chunk, per_chunk)].astype(jnp.float32)
            summed = summed + jnp.dot(
                attended.reshape(chunk, heads_width).astype(jnp.bfloat16), out_weight(1, part),
                preferred_element_type=jnp.float32,
            ).astype(jnp.bfloat16).astype(jnp.float32)
        stream[span, :] = stream[span, :] + mods[1, 2:3] * summed
        result_copy(index).start()
        return carry

    lax.fori_loop(0, chunks, time_project, 0)

    def drain(i, carry):
        kv_copy(i).wait_send()
        for distance in range(1, parts):
            h_copy(i, distance).wait_send()
        result_copy(i).wait()
        return carry

    lax.fori_loop(0, chunks, drain, 0)

    def drain_steps(i, carry):
        for distance in range(1, parts):
            part_copy(i, distance).wait_send()
        return carry

    lax.fori_loop(0, STEPS, drain_steps, 0)

    def drain_blocks(i, carry):
        for distance in range(1, parts):
            att_space_copy(i, distance).wait_send()
        return carry

    lax.fori_loop(0, query_blocks, drain_blocks, 0)

    def drain_pieces(i, carry):
        for distance in range(1, parts):
            att_time_copy(i, distance).wait_send()
        return carry

    lax.fori_loop(0, frames, drain_pieces, 0)

    def drain_other(target):
        tq_copy(target).wait_send()
        ta_copy(target).wait_send()

    others(drain_other)
    for distance in range(1, parts):
        for layer in range(2):
            stat_copy(layer, distance).wait_send()
        for kind in range(3):
            weight_copy(kind, distance).wait_send()
            core_copy(kind, distance).wait_send()
            for step in range(half_ring):
                twin_copy(kind, distance, step, place).wait_send()
                if step:
                    ring_copy(kind, distance, step, place).wait_send()


def on_device(tokens, block_mask, space_qkv, space_out, space_mod, time_qkv, time_out, time_mod):
    videos, rows, part_width = tokens.shape
    heads_width = space_qkv.shape[2]
    frames = lax.axis_size("seq") // 2
    parts = lax.axis_size("fsdp")
    piece = rows // frames
    chunk = piece if piece % 16 == 0 else 2 * piece
    chunks = rows // chunk
    blocks = rows // BLOCK
    width = part_width * parts
    bf16, f32 = jnp.bfloat16, jnp.float32
    dma = pltpu.SemaphoreType.DMA
    cut_rows = lambda weight: weight.reshape(RING, 2, heads_width // (2 * RING), width)
    hbm = pl.BlockSpec(memory_space=pl.ANY)
    scratch = [
        pltpu.VMEM((rows, part_width), f32),
        pltpu.VMEM((rows, 128), f32),
        pltpu.VMEM((rows, 3 * heads_width), f32),
        pltpu.VMEM((rows, heads_width), bf16),
        pltpu.VMEM((2, 2, rows, heads_width), bf16),
        pltpu.VMEM((rows, heads_width), f32),
        pltpu.VMEM((frames, piece, 3 * heads_width), bf16),
        pltpu.VMEM((frames, piece, 3 * heads_width), bf16),
        pltpu.VMEM((frames, piece, heads_width), bf16),
        pltpu.VMEM((width, 3 * heads_width), bf16),
        pltpu.VMEM((parts, 3, part_width, heads_width), bf16),
        pltpu.VMEM((2, parts, RING, 2, heads_width // (2 * RING), part_width), bf16),
        pltpu.VMEM((2, 3, part_width), f32),
        pltpu.VMEM((2, parts, 8, rows), f32),
        pltpu.VMEM((parts, rows, part_width), bf16),
        pltpu.VMEM((rows, part_width), bf16),
        pltpu.VMEM((parts, rows, 3 * heads_width), bf16),
        pltpu.VMEM((parts, rows, 3 * heads_width), bf16),
        pltpu.VMEM((parts, rows, heads_width), bf16),
        pltpu.VMEM((parts, frames, piece, heads_width), bf16),
        dma, dma((3,)), dma, dma((2,)), dma((2,)), dma((chunks,)),
        dma((2, parts)), dma((2, parts)),
        dma((parts, chunks)), dma((parts, chunks)),
        dma((parts, STEPS)), dma((parts, STEPS)),
        dma((chunks,)), dma((chunks,)),
        dma((parts, blocks)), dma((parts, blocks)),
        dma((parts, frames)), dma((parts, frames)),
        dma((3, parts)), dma((3, parts)),
        dma((3, parts, RING)), dma((3, parts, RING)),
        dma((3, parts)), dma((3, parts)),
        dma((frames,)), dma((frames,)),
        dma((frames,)), dma((frames,)),
    ]
    sizes = (frames, parts, rows, part_width, heads_width, chunk)
    return pl.pallas_call(
        functools.partial(sublayers, sizes),
        out_shape=jax.ShapeDtypeStruct(tokens.shape, f32),
        in_specs=[pl.BlockSpec(memory_space=pltpu.SMEM)] + [hbm] * 7,
        out_specs=hbm,
        scratch_shapes=scratch,
        compiler_params=pltpu.CompilerParams(
            collective_id=0, has_side_effects=True, vmem_limit_bytes=58 * 1024 * 1024
        ),
        cost_estimate=pl.CostEstimate(
            flops=4 * rows * width * 4 * heads_width, bytes_accessed=20 * 1024 * 1024,
            transcendentals=1024 * 1024,
        ),
    )(
        jnp.swapaxes(block_mask, 0, 1), tokens, jnp.swapaxes(space_qkv, 0, 1), cut_rows(space_out), space_mod,
        jnp.swapaxes(time_qkv, 0, 1), cut_rows(time_out), time_mod,
    )


def solution(mesh):
    placed = (
        P(None, "seq", "fsdp"),
        P(),
        P(None, None, "fsdp"),
        P("fsdp", None),
        P(),
        P(None, None, "fsdp"),
        P("fsdp", None),
        P(),
    )
    return jax.shard_map(
        on_device, mesh=mesh, in_specs=placed, out_specs=P(None, "seq", "fsdp"), check_vma=False
    )
```

```python
import functools
import math

import jax
import jax.numpy as jnp
from jax import lax
from jax.experimental import pallas as pl
from jax.experimental.pallas import tpu as pltpu
from jax.sharding import PartitionSpec as P

HD = 128
BLOCK = 128
EPS = 1e-06
RING = 8
STEPS = 4
MESH = pl.DeviceIdType.MESH
NT = (((1,), (1,)), ((), ()))


def softmax_rounded(scores):
    row_max = jnp.max(scores, axis=1, keepdims=True)
    lifted = jnp.exp(scores - row_max)
    return (lifted * (1.0 / jnp.sum(lifted, axis=1, keepdims=True))).astype(jnp.bfloat16)


def sublayers(
    sizes,
    mask_ref, tokens_ref, space_qkv_ref, space_out_ref, space_mod_ref, time_qkv_ref, time_out_ref,
    time_mod_ref, result_ref,
    stream, cols, total, queries, keys_values, sent_qkv, got_qkv, sent_att,
    space_w, cross_w, out_w, mods, stats, normed, h_time, part_sent, part_got, att_space, att_time,
    in_sem, w_sem, x_sem, o_sem, m_sem, out_sem,
    stat_s, stat_r, h_s, h_r, p_s, p_r, kv_s, kv_r, as_s, as_r, at_s, at_r,
    wq_s, wq_r, wf_s, wf_r, wc_s, wc_r, tq_s, tq_r, ta_s, ta_r,
):
    frames, parts, rows, part_width, heads_width, chunk = sizes
    chunks = rows // chunk
    piece = rows // frames
    per_chunk = chunk // piece
    step_rows = rows // STEPS
    per_step = step_rows // piece
    query_blocks = rows // BLOCK
    local_heads = heads_width // HD
    width = part_width * parts
    slab = part_width // RING
    lane_count = heads_width // 2
    scale = 1.0 / math.sqrt(HD)

    seq = lax.axis_index("seq")
    me = lax.axis_index("fsdp")
    half = lax.rem(seq, 2)
    frame = seq // 2
    place = lax.rem(frame, RING)
    base = frame - place

    def peer(distance):
        return lax.rem(me + distance, parts)

    def source(distance):
        return lax.rem(me + parts - distance, parts)

    def fsdp_copy(src, dst, send, recv, distance):
        return pltpu.make_async_remote_copy(
            src_ref=src, dst_ref=dst, send_sem=send, recv_sem=recv,
            device_id={"fsdp": peer(distance)}, device_id_type=MESH,
        )

    def seq_copy(src, dst, send, recv, target):
        return pltpu.make_async_remote_copy(
            src_ref=src, dst_ref=dst, send_sem=send, recv_sem=recv,
            device_id={"seq": target}, device_id_type=MESH,
        )

    out_refs = (space_out_ref, time_out_ref)
    mod_refs = (space_mod_ref, time_mod_ref)
    own_columns = pl.ds(pl.multiple_of(me * part_width, 128), part_width)
    other_core = seq + 1 - 2 * half

    def load_tokens():
        return pltpu.make_async_copy(tokens_ref.at[0], stream, in_sem)

    def load_space(kind):
        lanes = pl.ds(kind * heads_width, heads_width)
        return pltpu.make_async_copy(
            space_qkv_ref.at[kind], space_w.at[:, lanes], w_sem.at[kind]
        )

    def load_time():
        return pltpu.make_async_copy(
            time_qkv_ref.at[:, own_columns], cross_w.at[me], x_sem
        )

    def load_out(layer):
        return pltpu.make_async_copy(
            out_refs[layer].at[:, :, :, own_columns], out_w.at[layer, me], o_sem.at[layer]
        )

    def load_mod(layer):
        return pltpu.make_async_copy(
            mod_refs[layer].at[:, own_columns], mods.at[layer], m_sem.at[layer]
        )

    load_tokens().start()
    for layer in range(2):
        load_mod(layer).start()
    for kind in range(3):
        load_space(kind).start()

    barrier = pltpu.get_barrier_semaphore()
    for distance in range(1, parts):
        pl.semaphore_signal(barrier, inc=1, device_id={"fsdp": peer(distance)}, device_id_type=MESH)
    for distance in range(1, frames):
        other = lax.rem(frame + distance, frames) * 2 + half
        pl.semaphore_signal(barrier, inc=1, device_id={"seq": other}, device_id_type=MESH)
    pl.semaphore_signal(barrier, inc=1, device_id={"seq": other_core}, device_id_type=MESH)
    pl.semaphore_wait(barrier, parts + frames - 1)

    def slab_rows(first):
        return pl.ds(pl.multiple_of(first, 16), slab)

    own_lanes = pl.ds(pl.multiple_of(half * lane_count, 128), lane_count)

    def weight_piece(kind, owner, index):
        if kind == 1:
            return cross_w.at[owner, :, slab_rows(index * slab), own_lanes]
        return out_w.at[kind // 2, owner, index, half]

    def weight_copy(kind, distance):
        target = peer(distance)
        if kind == 1:
            first = target * part_width + place * slab
            block = time_qkv_ref.at[:, slab_rows(first), own_lanes]
        else:
            columns = pl.ds(pl.multiple_of(target * part_width, 128), part_width)
            block = out_refs[kind // 2].at[place, half, :, columns]
        return fsdp_copy(
            block, weight_piece(kind, me, place),
            wq_s.at[kind, distance], wq_r.at[kind, distance], distance,
        )

    twin = place + 1 - 2 * lax.rem(place, 2)
    half_ring = RING // 2

    def place_copy(kind, distance, slot, index, target):
        block = weight_piece(kind, source(distance), index)
        return seq_copy(
            block, block, wf_s.at[kind, distance, slot], wf_r.at[kind, distance, slot],
            (base + target) * 2 + half,
        )

    def ring_copy(kind, distance, step, index):
        return place_copy(kind, distance, step, index, lax.rem(place + 2 * step, RING))

    def twin_copy(kind, distance, step, own):
        index = lax.rem(own + RING - 2 * step, RING)
        return place_copy(kind, distance, half_ring + step, index, twin)

    def core_copy(kind, distance):
        owner = source(distance)
        if kind == 1:
            block = cross_w.at[owner, :, :, own_lanes]
        else:
            block = out_w.at[kind // 2, owner, :, half]
        return seq_copy(
            block, block, wc_s.at[kind, distance], wc_r.at[kind, distance], other_core
        )

    def fetch_weights(kind):
        for distance in range(1, parts):
            weight_copy(kind, distance).start()

    def pass_weights(kind):
        for distance in range(1, parts):
            weight_copy(kind, distance).wait_recv()
            for step in range(1, half_ring):
                ring_copy(kind, distance, step, place).start()
            twin_copy(kind, distance, 0, place).start()

    def relay_weights(kind):
        for distance in range(1, parts):
            for step in range(1, half_ring):
                ring_copy(kind, distance, step, lax.rem(place + RING - 2 * step, RING)).wait_recv()
                twin_copy(kind, distance, step, place).start()

    def swap_weights(kind):
        for distance in range(1, parts):
            for step in range(half_ring):
                twin_copy(kind, distance, step, twin).wait_recv()
            core_copy(kind, distance).start()

    def finish_weights(kind):
        for distance in range(1, parts):
            core_copy(kind, distance).wait_recv()

    def out_weight(layer, part):
        return out_w[layer, part].reshape(heads_width, part_width)

    def note_statistics(values, start, count):
        centre = jnp.sum(values, axis=1, keepdims=True) * (1.0 / part_width)
        offset = values - centre
        spread = jnp.sum(offset * offset, axis=1, keepdims=True)
        lane = lax.broadcasted_iota(jnp.int32, (count, 128), 1)
        cols[pl.ds(start, count), :] = jnp.where(lane == 0, centre, spread)

    def stat_copy(layer, distance):
        return fsdp_copy(
            stats.at[layer, me], stats.at[layer, me],
            stat_s.at[layer, distance], stat_r.at[layer, distance], distance,
        )

    def send_statistics(layer):
        stats[layer, me] = jnp.transpose(cols[...])[:8]
        for distance in range(1, parts):
            stat_copy(layer, distance).start()

    def finish_statistics(layer):
        for distance in range(1, parts):
            stat_copy(layer, distance).wait_recv()
        centre = jnp.zeros((1, rows), jnp.float32)
        for part in range(parts):
            centre = centre + stats[layer, part][0:1]
        centre = centre * (1.0 / parts)
        spread = jnp.zeros((1, rows), jnp.float32)
        for part in range(parts):
            shift = stats[layer, part][0:1] - centre
            spread = spread + stats[layer, part][1:2] * (1.0 / part_width) + shift * shift
        inverse = lax.rsqrt(spread * (1.0 / parts) + EPS)
        line = lax.broadcasted_iota(jnp.int32, (128, rows), 0)
        cols[...] = jnp.transpose(jnp.where(line == 0, centre, inverse))

    def chunk_rows(index):
        return pl.ds(pl.multiple_of(index * chunk, chunk), chunk)

    def block_rows(index):
        return pl.ds(pl.multiple_of(index * BLOCK, BLOCK), BLOCK)

    def h_copy(index, distance):
        block = normed.at[me, chunk_rows(index)]
        return fsdp_copy(
            block, block, h_s.at[distance, index], h_r.at[distance, index], distance
        )

    def normalised(layer, span):
        line = cols[span, :]
        shift = mods[layer, 0:1]
        gain = 1.0 + mods[layer, 1:2]
        values = (stream[span, :] - line[:, 0:1]) * line[:, 1:2] * gain + shift
        return values.astype(jnp.bfloat16)

    load_tokens().wait()

    def first_statistics(i, carry):
        start = pl.multiple_of(i * chunk, chunk)
        note_statistics(stream[pl.ds(start, chunk), :], start, chunk)
        return carry

    lax.fori_loop(0, chunks, first_statistics, 0)
    send_statistics(0)
    for kind in range(3):
        fetch_weights(kind)
    for layer in range(2):
        load_mod(layer).wait()
    load_time().start()
    load_out(0).start()
    load_out(1).start()
    finish_statistics(0)

    def space_send(index, carry):
        span = chunk_rows(index)
        normed[me, span, :] = normalised(0, span)
        for distance in range(1, parts):
            h_copy(index, distance).start()
        return carry

    lax.fori_loop(0, chunks, space_send, 0)
    for kind in range(3):
        pass_weights(kind)
    for kind in range(3):
        load_space(kind).wait()

    def space_depth(owner):
        return pl.ds(pl.multiple_of(owner * part_width, 128), part_width)

    def space_own(index, carry):
        span = block_rows(index)
        total[span, :] = jnp.dot(
            normed[me, span, :], space_w[space_depth(me), :], preferred_element_type=jnp.float32
        )
        return carry

    lax.fori_loop(0, query_blocks, space_own, 0)

    def kv_copy(index):
        block = keys_values.at[half, :, chunk_rows(index)]
        return seq_copy(block, block, kv_s.at[index], kv_r.at[index], other_core)

    def space_chunk(index, carry):
        span = chunk_rows(index)
        value = total[span, :]
        for distance in range(1, parts):
            h_copy(index, distance).wait_recv()
            other = source(distance)
            value = value + jnp.dot(
                normed[other, span, :], space_w[space_depth(other), :],
                preferred_element_type=jnp.float32,
            )
        value = value.astype(jnp.bfloat16)
        queries[span, :] = value[:, :heads_width]
        for kind in range(2):
            first = (kind + 1) * heads_width
            keys_values[half, kind, span, :] = value[:, first:first + heads_width]
        kv_copy(index).start()
        return carry

    relay_weights(0)
    lax.fori_loop(0, chunks // 2, space_chunk, 0)
    swap_weights(0)
    relay_weights(1)
    lax.fori_loop(chunks // 2, chunks, space_chunk, 0)

    def wait_keys(index, carry):
        kv_copy(index).wait_recv()
        return carry

    lax.fori_loop(0, chunks, wait_keys, 0)

    def att_space_copy(index, distance):
        block = att_space.at[me, block_rows(index)]
        return fsdp_copy(
            block, block, as_s.at[distance, index], as_r.at[distance, index], distance
        )

    def space_attention(index, carry):
        span = block_rows(index)
        bias = []
        for key_block in range(2 * query_blocks):
            kept = mask_ref[half * query_blocks + index, frame, key_block]
            bias.append(jnp.full((1, BLOCK), jnp.where(kept == 1, 0.0, -jnp.inf), jnp.float32))
        bias = jnp.concatenate(bias, axis=1)
        for head in range(local_heads):
            lanes = slice(head * HD, (head + 1) * HD)
            keys = keys_values[:, 0, :, lanes].reshape(2 * rows, HD)
            values = keys_values[:, 1, :, lanes].reshape(2 * rows, HD)
            scores = lax.dot_general(
                queries[span, lanes], keys, NT, preferred_element_type=jnp.float32
            )
            weights = softmax_rounded(scores * scale + bias)
            att_space[me, span, lanes] = jnp.dot(
                weights, values, preferred_element_type=jnp.float32
            ).astype(jnp.bfloat16)
        for distance in range(1, parts):
            att_space_copy(index, distance).start()
        return carry

    lax.fori_loop(0, query_blocks, space_attention, 0)
    relay_weights(2)
    swap_weights(1)
    load_out(0).wait()
    finish_weights(0)

    def space_project(index, carry):
        span = block_rows(index)
        for distance in range(1, parts):
            att_space_copy(index, distance).wait_recv()
        summed = jnp.zeros((BLOCK, part_width), jnp.float32)
        for part in range(parts):
            summed = summed + jnp.dot(
                att_space[part, span, :], out_weight(0, part), preferred_element_type=jnp.float32
            ).astype(jnp.bfloat16).astype(jnp.float32)
        values = stream[span, :] + mods[0, 2:3] * summed
        stream[span, :] = values
        note_statistics(values, pl.multiple_of(index * BLOCK, BLOCK), BLOCK)
        return carry

    lax.fori_loop(0, query_blocks, space_project, 0)

    send_statistics(1)
    load_time().wait()
    finish_statistics(1)
    finish_weights(1)

    def time_order(i):
        return lax.rem(frame // per_step + 1 + i, STEPS)

    def step_span(index):
        return pl.ds(pl.multiple_of(index * step_rows, step_rows), step_rows)

    def part_copy(index, distance):
        span = step_span(index)
        return fsdp_copy(
            part_sent.at[distance, span], part_got.at[distance, span],
            p_s.at[distance, index], p_r.at[distance, index], distance,
        )

    def kind_lanes(kind):
        return slice(kind * heads_width, (kind + 1) * heads_width)

    def time_send(i):
        index = time_order(i)
        span = step_span(index)
        values = normalised(1, span)
        h_time[span, :] = values
        for distance in range(1, parts):
            for kind in range(3):
                part_sent[distance, span, kind_lanes(kind)] = jnp.dot(
                    values, cross_w[peer(distance), kind], preferred_element_type=jnp.float32
                ).astype(jnp.bfloat16)
            part_copy(index, distance).start()
        for kind in range(3):
            total[span, kind_lanes(kind)] = jnp.dot(
                h_time[span, :], cross_w[me, kind], preferred_element_type=jnp.float32
            )

    def tq_copy(target):
        return seq_copy(
            sent_qkv.at[target], got_qkv.at[frame], tq_s.at[target], tq_r.at[frame],
            target * 2 + half,
        )

    def tq_arrival(origin):
        return seq_copy(
            sent_qkv.at[origin], got_qkv.at[origin], tq_s.at[origin], tq_r.at[origin],
            origin * 2 + half,
        )

    def time_pass(i):
        index = time_order(i)
        span = step_span(index)
        whole = total[span, :]
        for distance in range(1, parts):
            part_copy(index, distance).wait_recv()
            whole = whole + part_got[distance, span, :].astype(jnp.float32)
        whole = whole.reshape(per_step, piece, 3 * heads_width).astype(jnp.bfloat16)
        for n in range(per_step):
            target = index * per_step + n
            sent_qkv[target] = whole[n]

            @pl.when(target != frame)
            def _():
                tq_copy(target).start()

    time_send(0)

    def time_step(i, carry):
        time_send(i)
        time_pass(i - 1)
        return carry

    lax.fori_loop(1, STEPS, time_step, 0)
    time_pass(STEPS - 1)
    got_qkv[frame] = sent_qkv[frame]

    def others(action):
        def step(i, carry):
            action(lax.rem(frame + frames - 1 - i, frames))
            return carry

        lax.fori_loop(0, frames - 1, step, 0)

    others(lambda origin: tq_arrival(origin).wait_recv())

    def position(index):
        passed = jnp.zeros_like(index)
        for n in range(1, frames):
            passed = passed + jnp.where(index >= n * piece, piece, 0)
        return index - passed

    def flat(first):
        return got_qkv[:, :, first:first + HD].astype(jnp.float32).reshape(rows, HD).astype(jnp.bfloat16)

    def ta_copy(target):
        return seq_copy(
            sent_att.at[target], att_time.at[me, frame], ta_s.at[target], ta_r.at[frame],
            target * 2 + half,
        )

    def ta_arrival(origin):
        return seq_copy(
            sent_att.at[origin], att_time.at[me, origin], ta_s.at[origin], ta_r.at[origin],
            origin * 2 + half,
        )

    def att_time_copy(index, distance):
        block = att_time.at[me, index]
        return fsdp_copy(
            block, block, at_s.at[distance, index], at_r.at[distance, index], distance
        )

    def forward(index):
        for distance in range(1, parts):
            att_time_copy(index, distance).start()

    column = position(lax.broadcasted_iota(jnp.int32, (1, rows), 1))
    line = position(lax.broadcasted_iota(jnp.int32, (step_rows, 1), 0))
    head_keys = [flat(heads_width + head * HD) for head in range(local_heads)]
    head_values = [flat(2 * heads_width + head * HD) for head in range(local_heads)]

    def time_attention(i, carry):
        first = time_order(i) * per_step
        mixed = []
        for head in range(local_heads):
            asked = got_qkv[pl.ds(first, per_step), :, head * HD:(head + 1) * HD]
            asked = asked.astype(jnp.float32).reshape(step_rows, HD).astype(jnp.bfloat16)
            scores = lax.dot_general(
                asked, head_keys[head], NT, preferred_element_type=jnp.float32
            ) * scale
            weights = softmax_rounded(jnp.where(line == column, scores, -jnp.inf))
            mixed.append(jnp.dot(weights, head_values[head], preferred_element_type=jnp.float32))
        mixed = jnp.concatenate(mixed, axis=1).reshape(per_step, piece, heads_width)
        mixed = mixed.astype(jnp.bfloat16)
        for n in range(per_step):
            target = first + n

            @pl.when(target != frame)
            def _():
                sent_att[target] = mixed[n]
                ta_copy(target).start()

            @pl.when(target == frame)
            def _():
                att_time[me, frame] = mixed[n]
                forward(frame)

        return carry

    lax.fori_loop(0, STEPS, time_attention, 0)
    swap_weights(2)

    def relay(origin):
        ta_arrival(origin).wait_recv()
        forward(origin)

    others(relay)
    load_out(1).wait()
    finish_weights(2)

    def result_copy(index):
        span = chunk_rows(index)
        return pltpu.make_async_copy(stream.at[span], result_ref.at[0, span], out_sem.at[index])

    def time_project(i, carry):
        index = lax.rem(frame // per_chunk + chunks - i, chunks)
        span = chunk_rows(index)
        for n in range(per_chunk):
            for distance in range(1, parts):
                att_time_copy(index * per_chunk + n, distance).wait_recv()
        summed = jnp.zeros((chunk, part_width), jnp.float32)
        for part in range(parts):
            attended = att_time[part, pl.ds(index * per_chunk, per_chunk)].astype(jnp.float32)
            summed = summed + jnp.dot(
                attended.reshape(chunk, heads_width).astype(jnp.bfloat16), out_weight(1, part),
                preferred_element_type=jnp.float32,
            ).astype(jnp.bfloat16).astype(jnp.float32)
        stream[span, :] = stream[span, :] + mods[1, 2:3] * summed
        result_copy(index).start()
        return carry

    lax.fori_loop(0, chunks, time_project, 0)

    def drain(i, carry):
        kv_copy(i).wait_send()
        for distance in range(1, parts):
            h_copy(i, distance).wait_send()
        result_copy(i).wait()
        return carry

    lax.fori_loop(0, chunks, drain, 0)

    def drain_steps(i, carry):
        for distance in range(1, parts):
            part_copy(i, distance).wait_send()
        return carry

    lax.fori_loop(0, STEPS, drain_steps, 0)

    def drain_blocks(i, carry):
        for distance in range(1, parts):
            att_space_copy(i, distance).wait_send()
        return carry

    lax.fori_loop(0, query_blocks, drain_blocks, 0)

    def drain_pieces(i, carry):
        for distance in range(1, parts):
            att_time_copy(i, distance).wait_send()
        return carry

    lax.fori_loop(0, frames, drain_pieces, 0)

    def drain_other(target):
        tq_copy(target).wait_send()
        ta_copy(target).wait_send()

    others(drain_other)
    for distance in range(1, parts):
        for layer in range(2):
            stat_copy(layer, distance).wait_send()
        for kind in range(3):
            weight_copy(kind, distance).wait_send()
            core_copy(kind, distance).wait_send()
            for step in range(half_ring):
                twin_copy(kind, distance, step, place).wait_send()
                if step:
                    ring_copy(kind, distance, step, place).wait_send()


def on_device(tokens, block_mask, space_qkv, space_out, space_mod, time_qkv, time_out, time_mod):
    videos, rows, part_width = tokens.shape
    heads_width = space_qkv.shape[2]
    frames = lax.axis_size("seq") // 2
    parts = lax.axis_size("fsdp")
    piece = rows // frames
    chunk = rows // STEPS
    chunks = rows // chunk
    blocks = rows // BLOCK
    width = part_width * parts
    bf16, f32 = jnp.bfloat16, jnp.float32
    dma = pltpu.SemaphoreType.DMA
    cut_rows = lambda weight: weight.reshape(RING, 2, heads_width // (2 * RING), width)
    hbm = pl.BlockSpec(memory_space=pl.ANY)
    scratch = [
        pltpu.VMEM((rows, part_width), f32),
        pltpu.VMEM((rows, 128), f32),
        pltpu.VMEM((rows, 3 * heads_width), f32),
        pltpu.VMEM((rows, heads_width), bf16),
        pltpu.VMEM((2, 2, rows, heads_width), bf16),
        pltpu.VMEM((frames, piece, 3 * heads_width), bf16),
        pltpu.VMEM((frames, piece, 3 * heads_width), bf16),
        pltpu.VMEM((frames, piece, heads_width), bf16),
        pltpu.VMEM((width, 3 * heads_width), bf16),
        pltpu.VMEM((parts, 3, part_width, heads_width), bf16),
        pltpu.VMEM((2, parts, RING, 2, heads_width // (2 * RING), part_width), bf16),
        pltpu.VMEM((2, 3, part_width), f32),
        pltpu.VMEM((2, parts, 8, rows), f32),
        pltpu.VMEM((parts, rows, part_width), bf16),
        pltpu.VMEM((rows, part_width), bf16),
        pltpu.VMEM((parts, rows, 3 * heads_width), bf16),
        pltpu.VMEM((parts, rows, 3 * heads_width), bf16),
        pltpu.VMEM((parts, rows, heads_width), bf16),
        pltpu.VMEM((parts, frames, piece, heads_width), bf16),
        dma, dma((3,)), dma, dma((2,)), dma((2,)), dma((chunks,)),
        dma((2, parts)), dma((2, parts)),
        dma((parts, chunks)), dma((parts, chunks)),
        dma((parts, STEPS)), dma((parts, STEPS)),
        dma((chunks,)), dma((chunks,)),
        dma((parts, blocks)), dma((parts, blocks)),
        dma((parts, frames)), dma((parts, frames)),
        dma((3, parts)), dma((3, parts)),
        dma((3, parts, RING)), dma((3, parts, RING)),
        dma((3, parts)), dma((3, parts)),
        dma((frames,)), dma((frames,)),
        dma((frames,)), dma((frames,)),
    ]
    sizes = (frames, parts, rows, part_width, heads_width, chunk)
    return pl.pallas_call(
        functools.partial(sublayers, sizes),
        out_shape=jax.ShapeDtypeStruct(tokens.shape, f32),
        in_specs=[pl.BlockSpec(memory_space=pltpu.SMEM)] + [hbm] * 7,
        out_specs=hbm,
        scratch_shapes=scratch,
        compiler_params=pltpu.CompilerParams(
            collective_id=0, has_side_effects=True, vmem_limit_bytes=58 * 1024 * 1024
        ),
        cost_estimate=pl.CostEstimate(
            flops=4 * rows * width * 4 * heads_width, bytes_accessed=20 * 1024 * 1024,
            transcendentals=1024 * 1024,
        ),
    )(
        jnp.swapaxes(block_mask, 0, 1), tokens, jnp.swapaxes(space_qkv, 0, 1), cut_rows(space_out), space_mod,
        jnp.swapaxes(time_qkv, 0, 1), cut_rows(time_out), time_mod,
    )


def solution(mesh):
    placed = (
        P(None, "seq", "fsdp"),
        P(),
        P(None, None, "fsdp"),
        P("fsdp", None),
        P(),
        P(None, None, "fsdp"),
        P("fsdp", None),
        P(),
    )
    return jax.shard_map(
        on_device, mesh=mesh, in_specs=placed, out_specs=P(None, "seq", "fsdp"), check_vma=False
    )
```

```python
import functools
import math

import jax
import jax.numpy as jnp
from jax import lax
from jax.experimental import pallas as pl
from jax.experimental.pallas import tpu as pltpu
from jax.sharding import PartitionSpec as P

HD = 128
BLOCK = 128
EPS = 1e-06
RING = 8
STEPS = 4
MESH = pl.DeviceIdType.MESH
NT = (((1,), (1,)), ((), ()))


def softmax_rounded(scores):
    row_max = jnp.max(scores, axis=1, keepdims=True)
    lifted = jnp.exp(scores - row_max)
    return (lifted * (1.0 / jnp.sum(lifted, axis=1, keepdims=True))).astype(jnp.bfloat16)


def sublayers(
    sizes,
    mask_ref, tokens_ref, space_qkv_ref, space_out_ref, space_mod_ref, time_qkv_ref, time_out_ref,
    time_mod_ref, result_ref,
    stream, cols, total, queries, keys_values, sent_qkv, got_qkv, sent_att,
    space_w, cross_w, out_w, mods, stats, normed, h_time, part_sent, part_got, att_space, att_time,
    in_sem, w_sem, x_sem, o_sem, m_sem, out_sem,
    stat_s, stat_r, h_s, h_r, p_s, p_r, kv_s, kv_r, as_s, as_r, at_s, at_r,
    wq_s, wq_r, wf_s, wf_r, wc_s, wc_r, tq_s, tq_r, ta_s, ta_r,
):
    frames, parts, rows, part_width, heads_width, chunk = sizes
    chunks = rows // chunk
    piece = rows // frames
    per_chunk = chunk // piece
    step_rows = rows // STEPS
    per_step = step_rows // piece
    query_blocks = rows // BLOCK
    local_heads = heads_width // HD
    width = part_width * parts
    slab = part_width // RING
    lane_count = heads_width // 2
    scale = 1.0 / math.sqrt(HD)

    seq = lax.axis_index("seq")
    me = lax.axis_index("fsdp")
    half = lax.rem(seq, 2)
    frame = seq // 2
    place = lax.rem(frame, RING)
    base = frame - place

    def peer(distance):
        return lax.rem(me + distance, parts)

    def source(distance):
        return lax.rem(me + parts - distance, parts)

    def fsdp_copy(src, dst, send, recv, distance):
        return pltpu.make_async_remote_copy(
            src_ref=src, dst_ref=dst, send_sem=send, recv_sem=recv,
            device_id={"fsdp": peer(distance)}, device_id_type=MESH,
        )

    def seq_copy(src, dst, send, recv, target):
        return pltpu.make_async_remote_copy(
            src_ref=src, dst_ref=dst, send_sem=send, recv_sem=recv,
            device_id={"seq": target}, device_id_type=MESH,
        )

    out_refs = (space_out_ref, time_out_ref)
    mod_refs = (space_mod_ref, time_mod_ref)
    own_columns = pl.ds(pl.multiple_of(me * part_width, 128), part_width)
    other_core = seq + 1 - 2 * half

    def load_tokens():
        return pltpu.make_async_copy(tokens_ref.at[0], stream, in_sem)

    def load_space(kind):
        lanes = pl.ds(kind * heads_width, heads_width)
        return pltpu.make_async_copy(
            space_qkv_ref.at[kind], space_w.at[:, lanes], w_sem.at[kind]
        )

    def load_time():
        return pltpu.make_async_copy(
            time_qkv_ref.at[:, own_columns], cross_w.at[me], x_sem
        )

    def load_out(layer):
        return pltpu.make_async_copy(
            out_refs[layer].at[:, :, :, own_columns], out_w.at[layer, me], o_sem.at[layer]
        )

    def load_mod(layer):
        return pltpu.make_async_copy(
            mod_refs[layer].at[:, own_columns], mods.at[layer], m_sem.at[layer]
        )

    load_tokens().start()
    for layer in range(2):
        load_mod(layer).start()
    for kind in range(3):
        load_space(kind).start()

    barrier = pltpu.get_barrier_semaphore()
    for distance in range(1, parts):
        pl.semaphore_signal(barrier, inc=1, device_id={"fsdp": peer(distance)}, device_id_type=MESH)
    for distance in range(1, frames):
        other = lax.rem(frame + distance, frames) * 2 + half
        pl.semaphore_signal(barrier, inc=1, device_id={"seq": other}, device_id_type=MESH)
    pl.semaphore_signal(barrier, inc=1, device_id={"seq": other_core}, device_id_type=MESH)
    pl.semaphore_wait(barrier, parts + frames - 1)

    def slab_rows(first):
        return pl.ds(pl.multiple_of(first, 16), slab)

    own_lanes = pl.ds(pl.multiple_of(half * lane_count, 128), lane_count)

    def weight_piece(kind, owner, index):
        if kind == 1:
            return cross_w.at[owner, :, slab_rows(index * slab), own_lanes]
        return out_w.at[kind // 2, owner, index, half]

    def weight_copy(kind, distance):
        target = peer(distance)
        if kind == 1:
            first = target * part_width + place * slab
            block = time_qkv_ref.at[:, slab_rows(first), own_lanes]
        else:
            columns = pl.ds(pl.multiple_of(target * part_width, 128), part_width)
            block = out_refs[kind // 2].at[place, half, :, columns]
        return fsdp_copy(
            block, weight_piece(kind, me, place),
            wq_s.at[kind, distance], wq_r.at[kind, distance], distance,
        )

    twin = place + 1 - 2 * lax.rem(place, 2)
    half_ring = RING // 2

    def place_copy(kind, distance, slot, index, target):
        block = weight_piece(kind, source(distance), index)
        return seq_copy(
            block, block, wf_s.at[kind, distance, slot], wf_r.at[kind, distance, slot],
            (base + target) * 2 + half,
        )

    def ring_copy(kind, distance, step, index):
        return place_copy(kind, distance, step, index, lax.rem(place + 2 * step, RING))

    def twin_copy(kind, distance, step, own):
        index = lax.rem(own + RING - 2 * step, RING)
        return place_copy(kind, distance, half_ring + step, index, twin)

    def core_copy(kind, distance):
        owner = source(distance)
        if kind == 1:
            block = cross_w.at[owner, :, :, own_lanes]
        else:
            block = out_w.at[kind // 2, owner, :, half]
        return seq_copy(
            block, block, wc_s.at[kind, distance], wc_r.at[kind, distance], other_core
        )

    def fetch_weights(kind):
        for distance in range(1, parts):
            weight_copy(kind, distance).start()

    def pass_weights(kind):
        for distance in range(1, parts):
            weight_copy(kind, distance).wait_recv()
            for step in range(1, half_ring):
                ring_copy(kind, distance, step, place).start()
            twin_copy(kind, distance, 0, place).start()

    def relay_weights(kind):
        for distance in range(1, parts):
            for step in range(1, half_ring):
                ring_copy(kind, distance, step, lax.rem(place + RING - 2 * step, RING)).wait_recv()
                twin_copy(kind, distance, step, place).start()

    def swap_weights(kind):
        for distance in range(1, parts):
            for step in range(half_ring):
                twin_copy(kind, distance, step, twin).wait_recv()
            core_copy(kind, distance).start()

    def finish_weights(kind):
        for distance in range(1, parts):
            core_copy(kind, distance).wait_recv()

    def out_weight(layer, part):
        return out_w[layer, part].reshape(heads_width, part_width)

    def note_statistics(values, start, count):
        centre = jnp.sum(values, axis=1, keepdims=True) * (1.0 / part_width)
        offset = values - centre
        spread = jnp.sum(offset * offset, axis=1, keepdims=True)
        lane = lax.broadcasted_iota(jnp.int32, (count, 128), 1)
        cols[pl.ds(start, count), :] = jnp.where(lane == 0, centre, spread)

    def stat_copy(layer, distance):
        return fsdp_copy(
            stats.at[layer, me], stats.at[layer, me],
            stat_s.at[layer, distance], stat_r.at[layer, distance], distance,
        )

    def send_statistics(layer):
        stats[layer, me] = jnp.transpose(cols[...])[:8]
        for distance in range(1, parts):
            stat_copy(layer, distance).start()

    def finish_statistics(layer):
        for distance in range(1, parts):
            stat_copy(layer, distance).wait_recv()
        centre = jnp.zeros((1, rows), jnp.float32)
        for part in range(parts):
            centre = centre + stats[layer, part][0:1]
        centre = centre * (1.0 / parts)
        spread = jnp.zeros((1, rows), jnp.float32)
        for part in range(parts):
            shift = stats[layer, part][0:1] - centre
            spread = spread + stats[layer, part][1:2] * (1.0 / part_width) + shift * shift
        inverse = lax.rsqrt(spread * (1.0 / parts) + EPS)
        line = lax.broadcasted_iota(jnp.int32, (128, rows), 0)
        cols[...] = jnp.transpose(jnp.where(line == 0, centre, inverse))

    def chunk_rows(index):
        return pl.ds(pl.multiple_of(index * chunk, chunk), chunk)

    def block_rows(index):
        return pl.ds(pl.multiple_of(index * BLOCK, BLOCK), BLOCK)

    def h_copy(index, distance):
        block = normed.at[me, chunk_rows(index)]
        return fsdp_copy(
            block, block, h_s.at[distance, index], h_r.at[distance, index], distance
        )

    def normalised(layer, span):
        line = cols[span, :]
        shift = mods[layer, 0:1]
        gain = 1.0 + mods[layer, 1:2]
        values = (stream[span, :] - line[:, 0:1]) * line[:, 1:2] * gain + shift
        return values.astype(jnp.bfloat16)

    load_tokens().wait()

    def first_statistics(i, carry):
        start = pl.multiple_of(i * chunk, chunk)
        note_statistics(stream[pl.ds(start, chunk), :], start, chunk)
        return carry

    lax.fori_loop(0, chunks, first_statistics, 0)
    send_statistics(0)
    for kind in range(2):
        fetch_weights(kind)
    for layer in range(2):
        load_mod(layer).wait()
    load_time().start()
    load_out(0).start()
    load_out(1).start()
    finish_statistics(0)

    def space_send(index, carry):
        span = chunk_rows(index)
        normed[me, span, :] = normalised(0, span)
        for distance in range(1, parts):
            h_copy(index, distance).start()
        return carry

    lax.fori_loop(0, chunks, space_send, 0)
    fetch_weights(2)
    for kind in range(2):
        pass_weights(kind)
    for kind in range(3):
        load_space(kind).wait()

    def space_depth(owner):
        return pl.ds(pl.multiple_of(owner * part_width, 128), part_width)

    def space_own(index, carry):
        span = block_rows(index)
        total[span, :] = jnp.dot(
            normed[me, span, :], space_w[space_depth(me), :], preferred_element_type=jnp.float32
        )
        return carry

    lax.fori_loop(0, query_blocks, space_own, 0)

    def kv_copy(index):
        block = keys_values.at[half, :, chunk_rows(index)]
        return seq_copy(block, block, kv_s.at[index], kv_r.at[index], other_core)

    def space_chunk(index, carry):
        span = chunk_rows(index)
        value = total[span, :]
        for distance in range(1, parts):
            h_copy(index, distance).wait_recv()
            other = source(distance)
            value = value + jnp.dot(
                normed[other, span, :], space_w[space_depth(other), :],
                preferred_element_type=jnp.float32,
            )
        value = value.astype(jnp.bfloat16)
        queries[span, :] = value[:, :heads_width]
        for kind in range(2):
            first = (kind + 1) * heads_width
            keys_values[half, kind, span, :] = value[:, first:first + heads_width]
        kv_copy(index).start()
        return carry

    relay_weights(0)
    lax.fori_loop(0, chunks // 2, space_chunk, 0)
    swap_weights(0)
    relay_weights(1)
    lax.fori_loop(chunks // 2, chunks, space_chunk, 0)

    def wait_keys(index, carry):
        kv_copy(index).wait_recv()
        return carry

    lax.fori_loop(0, chunks, wait_keys, 0)

    def att_space_copy(index, distance):
        block = att_space.at[me, block_rows(index)]
        return fsdp_copy(
            block, block, as_s.at[distance, index], as_r.at[distance, index], distance
        )

    def space_attention(index, carry):
        span = block_rows(index)
        bias = []
        for key_block in range(2 * query_blocks):
            kept = mask_ref[half * query_blocks + index, frame, key_block]
            bias.append(jnp.full((1, BLOCK), jnp.where(kept == 1, 0.0, -jnp.inf), jnp.float32))
        bias = jnp.concatenate(bias, axis=1)
        for head in range(local_heads):
            lanes = slice(head * HD, (head + 1) * HD)
            keys = keys_values[:, 0, :, lanes].reshape(2 * rows, HD)
            values = keys_values[:, 1, :, lanes].reshape(2 * rows, HD)
            scores = lax.dot_general(
                queries[span, lanes], keys, NT, preferred_element_type=jnp.float32
            )
            weights = softmax_rounded(scores * scale + bias)
            att_space[me, span, lanes] = jnp.dot(
                weights, values, preferred_element_type=jnp.float32
            ).astype(jnp.bfloat16)
        for distance in range(1, parts):
            att_space_copy(index, distance).start()
        return carry

    lax.fori_loop(0, query_blocks, space_attention, 0)
    pass_weights(2)
    swap_weights(1)
    load_out(0).wait()
    finish_weights(0)

    def space_project(index, carry):
        span = block_rows(index)
        summed = jnp.zeros((BLOCK, part_width), jnp.float32)
        for distance in range(parts):
            part = source(distance)
            if distance:
                att_space_copy(index, distance).wait_recv()
            summed = summed + jnp.dot(
                att_space[part, span, :], out_weight(0, part), preferred_element_type=jnp.float32
            ).astype(jnp.bfloat16).astype(jnp.float32)
        values = stream[span, :] + mods[0, 2:3] * summed
        stream[span, :] = values
        note_statistics(values, pl.multiple_of(index * BLOCK, BLOCK), BLOCK)
        return carry

    lax.fori_loop(0, query_blocks, space_project, 0)

    send_statistics(1)
    load_time().wait()
    finish_statistics(1)
    finish_weights(1)

    def time_order(i):
        return lax.rem(frame // per_step + 1 + i, STEPS)

    def step_span(index):
        return pl.ds(pl.multiple_of(index * step_rows, step_rows), step_rows)

    def part_copy(index, distance):
        span = step_span(index)
        return fsdp_copy(
            part_sent.at[distance, span], part_got.at[distance, span],
            p_s.at[distance, index], p_r.at[distance, index], distance,
        )

    def kind_lanes(kind):
        return slice(kind * heads_width, (kind + 1) * heads_width)

    def time_send(i):
        index = time_order(i)
        span = step_span(index)
        values = normalised(1, span)
        h_time[span, :] = values
        for distance in range(1, parts):
            for kind in range(3):
                part_sent[distance, span, kind_lanes(kind)] = jnp.dot(
                    values, cross_w[peer(distance), kind], preferred_element_type=jnp.float32
                ).astype(jnp.bfloat16)
            part_copy(index, distance).start()
        for kind in range(3):
            total[span, kind_lanes(kind)] = jnp.dot(
                h_time[span, :], cross_w[me, kind], preferred_element_type=jnp.float32
            )

    def tq_copy(target):
        return seq_copy(
            sent_qkv.at[target], got_qkv.at[frame], tq_s.at[target], tq_r.at[frame],
            target * 2 + half,
        )

    def tq_arrival(origin):
        return seq_copy(
            sent_qkv.at[origin], got_qkv.at[origin], tq_s.at[origin], tq_r.at[origin],
            origin * 2 + half,
        )

    def time_pass(i):
        index = time_order(i)
        span = step_span(index)
        whole = total[span, :]
        for distance in range(1, parts):
            part_copy(index, distance).wait_recv()
            whole = whole + part_got[distance, span, :].astype(jnp.float32)
        whole = whole.reshape(per_step, piece, 3 * heads_width).astype(jnp.bfloat16)
        for n in range(per_step):
            target = index * per_step + n
            sent_qkv[target] = whole[n]

            @pl.when(target != frame)
            def _():
                tq_copy(target).start()

    time_send(0)

    def time_step(i, carry):
        time_send(i)
        time_pass(i - 1)
        return carry

    lax.fori_loop(1, STEPS, time_step, 0)
    time_pass(STEPS - 1)
    relay_weights(2)
    got_qkv[frame] = sent_qkv[frame]

    def others(action):
        def step(i, carry):
            action(lax.rem(frame + frames - 1 - i, frames))
            return carry

        lax.fori_loop(0, frames - 1, step, 0)

    others(lambda origin: tq_arrival(origin).wait_recv())

    def position(index):
        passed = jnp.zeros_like(index)
        for n in range(1, frames):
            passed = passed + jnp.where(index >= n * piece, piece, 0)
        return index - passed

    def flat(first):
        return got_qkv[:, :, first:first + HD].astype(jnp.float32).reshape(rows, HD).astype(jnp.bfloat16)

    def ta_copy(target):
        return seq_copy(
            sent_att.at[target], att_time.at[me, frame], ta_s.at[target], ta_r.at[frame],
            target * 2 + half,
        )

    def ta_arrival(origin):
        return seq_copy(
            sent_att.at[origin], att_time.at[me, origin], ta_s.at[origin], ta_r.at[origin],
            origin * 2 + half,
        )

    def att_time_copy(index, distance):
        block = att_time.at[me, index]
        return fsdp_copy(
            block, block, at_s.at[distance, index], at_r.at[distance, index], distance
        )

    def forward(index):
        for distance in range(1, parts):
            att_time_copy(index, distance).start()

    column = position(lax.broadcasted_iota(jnp.int32, (1, rows), 1))
    line = position(lax.broadcasted_iota(jnp.int32, (step_rows, 1), 0))
    head_keys = [flat(heads_width + head * HD) for head in range(local_heads)]
    head_values = [flat(2 * heads_width + head * HD) for head in range(local_heads)]

    def time_attention(i, carry):
        first = time_order(i) * per_step
        mixed = []
        for head in range(local_heads):
            asked = got_qkv[pl.ds(first, per_step), :, head * HD:(head + 1) * HD]
            asked = asked.astype(jnp.float32).reshape(step_rows, HD).astype(jnp.bfloat16)
            scores = lax.dot_general(
                asked, head_keys[head], NT, preferred_element_type=jnp.float32
            ) * scale
            weights = softmax_rounded(jnp.where(line == column, scores, -jnp.inf))
            mixed.append(jnp.dot(weights, head_values[head], preferred_element_type=jnp.float32))
        mixed = jnp.concatenate(mixed, axis=1).reshape(per_step, piece, heads_width)
        mixed = mixed.astype(jnp.bfloat16)
        for n in range(per_step):
            target = first + n

            @pl.when(target != frame)
            def _():
                sent_att[target] = mixed[n]
                ta_copy(target).start()

            @pl.when(target == frame)
            def _():
                att_time[me, frame] = mixed[n]
                forward(frame)

        return carry

    lax.fori_loop(0, STEPS, time_attention, 0)
    swap_weights(2)

    def relay(origin):
        ta_arrival(origin).wait_recv()
        forward(origin)

    others(relay)
    load_out(1).wait()
    finish_weights(2)

    def result_copy(index):
        span = chunk_rows(index)
        return pltpu.make_async_copy(stream.at[span], result_ref.at[0, span], out_sem.at[index])

    def time_project(i, carry):
        index = lax.rem(frame // per_chunk + chunks - i, chunks)
        span = chunk_rows(index)
        for n in range(per_chunk):
            for distance in range(1, parts):
                att_time_copy(index * per_chunk + n, distance).wait_recv()
        summed = jnp.zeros((chunk, part_width), jnp.float32)
        for part in range(parts):
            attended = att_time[part, pl.ds(index * per_chunk, per_chunk)].astype(jnp.float32)
            summed = summed + jnp.dot(
                attended.reshape(chunk, heads_width).astype(jnp.bfloat16), out_weight(1, part),
                preferred_element_type=jnp.float32,
            ).astype(jnp.bfloat16).astype(jnp.float32)
        stream[span, :] = stream[span, :] + mods[1, 2:3] * summed
        result_copy(index).start()
        return carry

    lax.fori_loop(0, chunks, time_project, 0)

    def drain(i, carry):
        kv_copy(i).wait_send()
        for distance in range(1, parts):
            h_copy(i, distance).wait_send()
        result_copy(i).wait()
        return carry

    lax.fori_loop(0, chunks, drain, 0)

    def drain_steps(i, carry):
        for distance in range(1, parts):
            part_copy(i, distance).wait_send()
        return carry

    lax.fori_loop(0, STEPS, drain_steps, 0)

    def drain_blocks(i, carry):
        for distance in range(1, parts):
            att_space_copy(i, distance).wait_send()
        return carry

    lax.fori_loop(0, query_blocks, drain_blocks, 0)

    def drain_pieces(i, carry):
        for distance in range(1, parts):
            att_time_copy(i, distance).wait_send()
        return carry

    lax.fori_loop(0, frames, drain_pieces, 0)

    def drain_other(target):
        tq_copy(target).wait_send()
        ta_copy(target).wait_send()

    others(drain_other)
    for distance in range(1, parts):
        for layer in range(2):
            stat_copy(layer, distance).wait_send()
        for kind in range(3):
            weight_copy(kind, distance).wait_send()
            core_copy(kind, distance).wait_send()
            for step in range(half_ring):
                twin_copy(kind, distance, step, place).wait_send()
                if step:
                    ring_copy(kind, distance, step, place).wait_send()


def on_device(tokens, block_mask, space_qkv, space_out, space_mod, time_qkv, time_out, time_mod):
    videos, rows, part_width = tokens.shape
    heads_width = space_qkv.shape[2]
    frames = lax.axis_size("seq") // 2
    parts = lax.axis_size("fsdp")
    piece = rows // frames
    chunk = rows // STEPS
    chunks = rows // chunk
    blocks = rows // BLOCK
    width = part_width * parts
    bf16, f32 = jnp.bfloat16, jnp.float32
    dma = pltpu.SemaphoreType.DMA
    cut_rows = lambda weight: weight.reshape(RING, 2, heads_width // (2 * RING), width)
    hbm = pl.BlockSpec(memory_space=pl.ANY)
    scratch = [
        pltpu.VMEM((rows, part_width), f32),
        pltpu.VMEM((rows, 128), f32),
        pltpu.VMEM((rows, 3 * heads_width), f32),
        pltpu.VMEM((rows, heads_width), bf16),
        pltpu.VMEM((2, 2, rows, heads_width), bf16),
        pltpu.VMEM((frames, piece, 3 * heads_width), bf16),
        pltpu.VMEM((frames, piece, 3 * heads_width), bf16),
        pltpu.VMEM((frames, piece, heads_width), bf16),
        pltpu.VMEM((width, 3 * heads_width), bf16),
        pltpu.VMEM((parts, 3, part_width, heads_width), bf16),
        pltpu.VMEM((2, parts, RING, 2, heads_width // (2 * RING), part_width), bf16),
        pltpu.VMEM((2, 3, part_width), f32),
        pltpu.VMEM((2, parts, 8, rows), f32),
        pltpu.VMEM((parts, rows, part_width), bf16),
        pltpu.VMEM((rows, part_width), bf16),
        pltpu.VMEM((parts, rows, 3 * heads_width), bf16),
        pltpu.VMEM((parts, rows, 3 * heads_width), bf16),
        pltpu.VMEM((parts, rows, heads_width), bf16),
        pltpu.VMEM((parts, frames, piece, heads_width), bf16),
        dma, dma((3,)), dma, dma((2,)), dma((2,)), dma((chunks,)),
        dma((2, parts)), dma((2, parts)),
        dma((parts, chunks)), dma((parts, chunks)),
        dma((parts, STEPS)), dma((parts, STEPS)),
        dma((chunks,)), dma((chunks,)),
        dma((parts, blocks)), dma((parts, blocks)),
        dma((parts, frames)), dma((parts, frames)),
        dma((3, parts)), dma((3, parts)),
        dma((3, parts, RING)), dma((3, parts, RING)),
        dma((3, parts)), dma((3, parts)),
        dma((frames,)), dma((frames,)),
        dma((frames,)), dma((frames,)),
    ]
    sizes = (frames, parts, rows, part_width, heads_width, chunk)
    return pl.pallas_call(
        functools.partial(sublayers, sizes),
        out_shape=jax.ShapeDtypeStruct(tokens.shape, f32),
        in_specs=[pl.BlockSpec(memory_space=pltpu.SMEM)] + [hbm] * 7,
        out_specs=hbm,
        scratch_shapes=scratch,
        compiler_params=pltpu.CompilerParams(
            collective_id=0, has_side_effects=True, vmem_limit_bytes=58 * 1024 * 1024
        ),
        cost_estimate=pl.CostEstimate(
            flops=4 * rows * width * 4 * heads_width, bytes_accessed=20 * 1024 * 1024,
            transcendentals=1024 * 1024,
        ),
    )(
        jnp.swapaxes(block_mask, 0, 1), tokens, jnp.swapaxes(space_qkv, 0, 1), cut_rows(space_out), space_mod,
        jnp.swapaxes(time_qkv, 0, 1), cut_rows(time_out), time_mod,
    )


def solution(mesh):
    placed = (
        P(None, "seq", "fsdp"),
        P(),
        P(None, None, "fsdp"),
        P("fsdp", None),
        P(),
        P(None, None, "fsdp"),
        P("fsdp", None),
        P(),
    )
    return jax.shard_map(
        on_device, mesh=mesh, in_specs=placed, out_specs=P(None, "seq", "fsdp"), check_vma=False
    )
```

```python
import functools
import math

import jax
import jax.numpy as jnp
from jax import lax
from jax.experimental import pallas as pl
from jax.experimental.pallas import tpu as pltpu
from jax.sharding import PartitionSpec as P

HD = 128
BLOCK = 128
EPS = 1e-06
RING = 8
STEPS = 4
MESH = pl.DeviceIdType.MESH
NT = (((1,), (1,)), ((), ()))


def softmax_rounded(scores):
    row_max = jnp.max(scores, axis=1, keepdims=True)
    lifted = jnp.exp(scores - row_max)
    return (lifted * (1.0 / jnp.sum(lifted, axis=1, keepdims=True))).astype(jnp.bfloat16)


def sublayers(
    sizes,
    mask_ref, tokens_ref, space_qkv_ref, space_out_ref, space_mod_ref, time_qkv_ref, time_out_ref,
    time_mod_ref, result_ref,
    stream, cols, total, queries, keys_values, sent_qkv, got_qkv, sent_att,
    space_w, cross_w, out_w, mods, stats, normed, h_time, part_sent, part_got, att_space, att_time,
    in_sem, w_sem, x_sem, o_sem, m_sem, out_sem,
    stat_s, stat_r, h_s, h_r, p_s, p_r, kv_s, kv_r, as_s, as_r, at_s, at_r,
    wq_s, wq_r, wf_s, wf_r, wc_s, wc_r, tq_s, tq_r, ta_s, ta_r,
):
    frames, parts, rows, part_width, heads_width, chunk = sizes
    chunks = rows // chunk
    piece = rows // frames
    per_chunk = chunk // piece
    step_rows = rows // STEPS
    per_step = step_rows // piece
    query_blocks = rows // BLOCK
    local_heads = heads_width // HD
    width = part_width * parts
    slab = part_width // RING
    lane_count = heads_width // 2
    scale = 1.0 / math.sqrt(HD)

    seq = lax.axis_index("seq")
    me = lax.axis_index("fsdp")
    half = lax.rem(seq, 2)
    frame = seq // 2
    place = lax.rem(frame, RING)
    base = frame - place

    def peer(distance):
        return lax.rem(me + distance, parts)

    def source(distance):
        return lax.rem(me + parts - distance, parts)

    def fsdp_copy(src, dst, send, recv, distance):
        return pltpu.make_async_remote_copy(
            src_ref=src, dst_ref=dst, send_sem=send, recv_sem=recv,
            device_id={"fsdp": peer(distance)}, device_id_type=MESH,
        )

    def seq_copy(src, dst, send, recv, target):
        return pltpu.make_async_remote_copy(
            src_ref=src, dst_ref=dst, send_sem=send, recv_sem=recv,
            device_id={"seq": target}, device_id_type=MESH,
        )

    out_refs = (space_out_ref, time_out_ref)
    mod_refs = (space_mod_ref, time_mod_ref)
    own_columns = pl.ds(pl.multiple_of(me * part_width, 128), part_width)
    other_core = seq + 1 - 2 * half

    def load_tokens():
        return pltpu.make_async_copy(tokens_ref.at[0], stream, in_sem)

    def load_space(kind):
        lanes = pl.ds(kind * heads_width, heads_width)
        return pltpu.make_async_copy(
            space_qkv_ref.at[kind], space_w.at[:, lanes], w_sem.at[kind]
        )

    def load_time():
        return pltpu.make_async_copy(
            time_qkv_ref.at[:, own_columns], cross_w.at[me], x_sem
        )

    def load_out(layer):
        return pltpu.make_async_copy(
            out_refs[layer].at[:, :, :, own_columns], out_w.at[layer, me], o_sem.at[layer]
        )

    def load_mod(layer):
        return pltpu.make_async_copy(
            mod_refs[layer].at[:, own_columns], mods.at[layer], m_sem.at[layer]
        )

    load_tokens().start()
    for layer in range(2):
        load_mod(layer).start()
    for kind in range(3):
        load_space(kind).start()

    barrier = pltpu.get_barrier_semaphore()
    for distance in range(1, parts):
        pl.semaphore_signal(barrier, inc=1, device_id={"fsdp": peer(distance)}, device_id_type=MESH)
    for distance in range(1, frames):
        other = lax.rem(frame + distance, frames) * 2 + half
        pl.semaphore_signal(barrier, inc=1, device_id={"seq": other}, device_id_type=MESH)
    pl.semaphore_signal(barrier, inc=1, device_id={"seq": other_core}, device_id_type=MESH)
    pl.semaphore_wait(barrier, parts + frames - 1)

    def slab_rows(first):
        return pl.ds(pl.multiple_of(first, 16), slab)

    own_lanes = pl.ds(pl.multiple_of(half * lane_count, 128), lane_count)

    def weight_piece(kind, owner, index):
        if kind == 1:
            return cross_w.at[owner, :, slab_rows(index * slab), own_lanes]
        return out_w.at[kind // 2, owner, index, half]

    def weight_copy(kind, distance):
        target = peer(distance)
        if kind == 1:
            first = target * part_width + place * slab
            block = time_qkv_ref.at[:, slab_rows(first), own_lanes]
        else:
            columns = pl.ds(pl.multiple_of(target * part_width, 128), part_width)
            block = out_refs[kind // 2].at[place, half, :, columns]
        return fsdp_copy(
            block, weight_piece(kind, me, place),
            wq_s.at[kind, distance], wq_r.at[kind, distance], distance,
        )

    twin = place + 1 - 2 * lax.rem(place, 2)
    half_ring = RING // 2

    def place_copy(kind, distance, slot, index, target):
        block = weight_piece(kind, source(distance), index)
        return seq_copy(
            block, block, wf_s.at[kind, distance, slot], wf_r.at[kind, distance, slot],
            (base + target) * 2 + half,
        )

    def ring_copy(kind, distance, step, index):
        return place_copy(kind, distance, step, index, lax.rem(place + 2 * step, RING))

    def twin_copy(kind, distance, step, own):
        index = lax.rem(own + RING - 2 * step, RING)
        return place_copy(kind, distance, half_ring + step, index, twin)

    def core_copy(kind, distance):
        owner = source(distance)
        if kind == 1:
            block = cross_w.at[owner, :, :, own_lanes]
        else:
            block = out_w.at[kind // 2, owner, :, half]
        return seq_copy(
            block, block, wc_s.at[kind, distance], wc_r.at[kind, distance], other_core
        )

    def fetch_weights(kind):
        for distance in range(1, parts):
            weight_copy(kind, distance).start()

    def pass_weights(kind):
        for distance in range(1, parts):
            weight_copy(kind, distance).wait_recv()
            for step in range(1, half_ring):
                ring_copy(kind, distance, step, place).start()
            twin_copy(kind, distance, 0, place).start()

    def relay_weights(kind):
        for distance in range(1, parts):
            for step in range(1, half_ring):
                ring_copy(kind, distance, step, lax.rem(place + RING - 2 * step, RING)).wait_recv()
                twin_copy(kind, distance, step, place).start()

    def swap_weights(kind):
        for distance in range(1, parts):
            for step in range(half_ring):
                twin_copy(kind, distance, step, twin).wait_recv()
            core_copy(kind, distance).start()

    def finish_weights(kind):
        for distance in range(1, parts):
            core_copy(kind, distance).wait_recv()

    def out_weight(layer, part):
        return out_w[layer, part].reshape(heads_width, part_width)

    def note_statistics(values, start, count):
        centre = jnp.sum(values, axis=1, keepdims=True) * (1.0 / part_width)
        offset = values - centre
        spread = jnp.sum(offset * offset, axis=1, keepdims=True)
        lane = lax.broadcasted_iota(jnp.int32, (count, 128), 1)
        cols[pl.ds(start, count), :] = jnp.where(lane == 0, centre, spread)

    def stat_copy(layer, distance):
        return fsdp_copy(
            stats.at[layer, me], stats.at[layer, me],
            stat_s.at[layer, distance], stat_r.at[layer, distance], distance,
        )

    def send_statistics(layer):
        stats[layer, me] = jnp.transpose(cols[...])[:8]
        for distance in range(1, parts):
            stat_copy(layer, distance).start()

    def finish_statistics(layer):
        for distance in range(1, parts):
            stat_copy(layer, distance).wait_recv()
        centre = jnp.zeros((1, rows), jnp.float32)
        for part in range(parts):
            centre = centre + stats[layer, part][0:1]
        centre = centre * (1.0 / parts)
        spread = jnp.zeros((1, rows), jnp.float32)
        for part in range(parts):
            shift = stats[layer, part][0:1] - centre
            spread = spread + stats[layer, part][1:2] * (1.0 / part_width) + shift * shift
        inverse = lax.rsqrt(spread * (1.0 / parts) + EPS)
        line = lax.broadcasted_iota(jnp.int32, (128, rows), 0)
        cols[...] = jnp.transpose(jnp.where(line == 0, centre, inverse))

    def chunk_rows(index):
        return pl.ds(pl.multiple_of(index * chunk, chunk), chunk)

    def block_rows(index):
        return pl.ds(pl.multiple_of(index * BLOCK, BLOCK), BLOCK)

    def h_copy(index, distance):
        block = normed.at[me, chunk_rows(index)]
        return fsdp_copy(
            block, block, h_s.at[distance, index], h_r.at[distance, index], distance
        )

    def normalised(layer, span):
        line = cols[span, :]
        shift = mods[layer, 0:1]
        gain = 1.0 + mods[layer, 1:2]
        values = (stream[span, :] - line[:, 0:1]) * line[:, 1:2] * gain + shift
        return values.astype(jnp.bfloat16)

    load_tokens().wait()

    def first_statistics(i, carry):
        start = pl.multiple_of(i * chunk, chunk)
        note_statistics(stream[pl.ds(start, chunk), :], start, chunk)
        return carry

    lax.fori_loop(0, chunks, first_statistics, 0)
    send_statistics(0)
    for kind in range(2):
        fetch_weights(kind)
    for layer in range(2):
        load_mod(layer).wait()
    load_time().start()
    load_out(0).start()
    load_out(1).start()
    finish_statistics(0)

    def space_send(index, carry):
        span = chunk_rows(index)
        normed[me, span, :] = normalised(0, span)
        for distance in range(1, parts):
            h_copy(index, distance).start()
        return carry

    lax.fori_loop(0, chunks, space_send, 0)
    fetch_weights(2)
    for kind in range(2):
        pass_weights(kind)
    for kind in range(3):
        load_space(kind).wait()

    def space_depth(owner):
        return pl.ds(pl.multiple_of(owner * part_width, 128), part_width)

    def space_own(index, carry):
        span = block_rows(index)
        total[span, :] = jnp.dot(
            normed[me, span, :], space_w[space_depth(me), :], preferred_element_type=jnp.float32
        )
        return carry

    lax.fori_loop(0, query_blocks, space_own, 0)

    def kv_copy(index):
        block = keys_values.at[half, :, chunk_rows(index)]
        return seq_copy(block, block, kv_s.at[index], kv_r.at[index], other_core)

    def space_chunk(index, carry):
        span = chunk_rows(index)
        value = total[span, :]
        for distance in range(1, parts):
            h_copy(index, distance).wait_recv()
            other = source(distance)
            value = value + jnp.dot(
                normed[other, span, :], space_w[space_depth(other), :],
                preferred_element_type=jnp.float32,
            )
        value = value.astype(jnp.bfloat16)
        queries[span, :] = value[:, :heads_width]
        for kind in range(2):
            first = (kind + 1) * heads_width
            keys_values[half, kind, span, :] = value[:, first:first + heads_width]
        kv_copy(index).start()
        return carry

    relay_weights(0)
    lax.fori_loop(0, chunks // 2, space_chunk, 0)
    swap_weights(0)
    relay_weights(1)
    lax.fori_loop(chunks // 2, chunks, space_chunk, 0)

    def wait_keys(index, carry):
        kv_copy(index).wait_recv()
        return carry

    lax.fori_loop(0, chunks, wait_keys, 0)

    def att_space_copy(index, distance):
        block = att_space.at[me, block_rows(index)]
        return fsdp_copy(
            block, block, as_s.at[distance, index], as_r.at[distance, index], distance
        )

    def space_attention(index, carry):
        span = block_rows(index)
        bias = []
        for key_block in range(2 * query_blocks):
            kept = mask_ref[half * query_blocks + index, frame, key_block]
            bias.append(jnp.full((1, BLOCK), jnp.where(kept == 1, 0.0, -jnp.inf), jnp.float32))
        bias = jnp.concatenate(bias, axis=1)
        for head in range(local_heads):
            lanes = slice(head * HD, (head + 1) * HD)
            keys = keys_values[:, 0, :, lanes].reshape(2 * rows, HD)
            values = keys_values[:, 1, :, lanes].reshape(2 * rows, HD)
            scores = lax.dot_general(
                queries[span, lanes], keys, NT, preferred_element_type=jnp.float32
            )
            weights = softmax_rounded(scores * scale + bias)
            att_space[me, span, lanes] = jnp.dot(
                weights, values, preferred_element_type=jnp.float32
            ).astype(jnp.bfloat16)
        for distance in range(1, parts):
            att_space_copy(index, distance).start()
        return carry

    lax.fori_loop(0, query_blocks, space_attention, 0)
    pass_weights(2)
    swap_weights(1)
    load_out(0).wait()
    finish_weights(0)

    def space_project(index, carry):
        span = block_rows(index)
        summed = jnp.zeros((BLOCK, part_width), jnp.float32)
        for distance in range(parts):
            part = source(distance)
            if distance:
                att_space_copy(index, distance).wait_recv()
            summed = summed + jnp.dot(
                att_space[part, span, :], out_weight(0, part), preferred_element_type=jnp.float32
            ).astype(jnp.bfloat16).astype(jnp.float32)
        values = stream[span, :] + mods[0, 2:3] * summed
        stream[span, :] = values
        note_statistics(values, pl.multiple_of(index * BLOCK, BLOCK), BLOCK)
        return carry

    lax.fori_loop(0, query_blocks, space_project, 0)

    send_statistics(1)
    load_time().wait()
    finish_statistics(1)
    finish_weights(1)

    def time_order(i):
        return lax.rem(frame // per_step + 1 + i, STEPS)

    def step_span(index):
        return pl.ds(pl.multiple_of(index * step_rows, step_rows), step_rows)

    def part_copy(index, distance):
        span = step_span(index)
        return fsdp_copy(
            part_sent.at[distance, span], part_got.at[distance, span],
            p_s.at[distance, index], p_r.at[distance, index], distance,
        )

    def kind_lanes(kind):
        return slice(kind * heads_width, (kind + 1) * heads_width)

    def time_send(i):
        index = time_order(i)
        span = step_span(index)
        values = normalised(1, span)
        h_time[span, :] = values
        for distance in range(1, parts):
            for kind in range(3):
                part_sent[distance, span, kind_lanes(kind)] = jnp.dot(
                    values, cross_w[peer(distance), kind], preferred_element_type=jnp.float32
                ).astype(jnp.bfloat16)
            part_copy(index, distance).start()
        for kind in range(3):
            total[span, kind_lanes(kind)] = jnp.dot(
                h_time[span, :], cross_w[me, kind], preferred_element_type=jnp.float32
            )

    def tq_copy(target):
        return seq_copy(
            sent_qkv.at[target], got_qkv.at[frame], tq_s.at[target], tq_r.at[frame],
            target * 2 + half,
        )

    def tq_arrival(origin):
        return seq_copy(
            sent_qkv.at[origin], got_qkv.at[origin], tq_s.at[origin], tq_r.at[origin],
            origin * 2 + half,
        )

    def time_pass(i):
        index = time_order(i)
        span = step_span(index)
        whole = total[span, :]
        for distance in range(1, parts):
            part_copy(index, distance).wait_recv()
            whole = whole + part_got[distance, span, :].astype(jnp.float32)
        whole = whole.reshape(per_step, piece, 3 * heads_width).astype(jnp.bfloat16)
        for n in range(per_step):
            target = index * per_step + n
            sent_qkv[target] = whole[n]

            @pl.when(target != frame)
            def _():
                tq_copy(target).start()

    time_send(0)

    def time_step(i, carry):
        time_send(i)
        time_pass(i - 1)
        return carry

    lax.fori_loop(1, STEPS, time_step, 0)
    time_pass(STEPS - 1)
    relay_weights(2)
    got_qkv[frame] = sent_qkv[frame]

    def others(action):
        def step(i, carry):
            action(lax.rem(frame + frames - 1 - i, frames))
            return carry

        lax.fori_loop(0, frames - 1, step, 0)

    others(lambda origin: tq_arrival(origin).wait_recv())

    def position(index):
        passed = jnp.zeros_like(index)
        for n in range(1, frames):
            passed = passed + jnp.where(index >= n * piece, piece, 0)
        return index - passed

    def flat(first):
        return got_qkv[:, :, first:first + HD].astype(jnp.float32).reshape(rows, HD).astype(jnp.bfloat16)

    def ta_copy(target):
        return seq_copy(
            sent_att.at[target], att_time.at[me, frame], ta_s.at[target], ta_r.at[frame],
            target * 2 + half,
        )

    def ta_arrival(origin):
        return seq_copy(
            sent_att.at[origin], att_time.at[me, origin], ta_s.at[origin], ta_r.at[origin],
            origin * 2 + half,
        )

    def att_time_copy(index, distance):
        block = att_time.at[me, index]
        return fsdp_copy(
            block, block, at_s.at[distance, index], at_r.at[distance, index], distance
        )

    def forward(index):
        for distance in range(1, parts):
            att_time_copy(index, distance).start()

    column = position(lax.broadcasted_iota(jnp.int32, (1, rows), 1))
    line = position(lax.broadcasted_iota(jnp.int32, (step_rows, 1), 0))
    head_keys = [flat(heads_width + head * HD) for head in range(local_heads)]
    head_values = [flat(2 * heads_width + head * HD) for head in range(local_heads)]

    def time_attention(i, carry):
        first = time_order(i) * per_step
        mixed = []
        for head in range(local_heads):
            asked = got_qkv[pl.ds(first, per_step), :, head * HD:(head + 1) * HD]
            asked = asked.astype(jnp.float32).reshape(step_rows, HD).astype(jnp.bfloat16)
            scores = lax.dot_general(
                asked, head_keys[head], NT, preferred_element_type=jnp.float32
            ) * scale
            weights = softmax_rounded(jnp.where(line == column, scores, -jnp.inf))
            mixed.append(jnp.dot(weights, head_values[head], preferred_element_type=jnp.float32))
        mixed = jnp.concatenate(mixed, axis=1).reshape(per_step, piece, heads_width)
        mixed = mixed.astype(jnp.bfloat16)
        for n in range(per_step):
            target = first + n

            @pl.when(target != frame)
            def _():
                sent_att[target] = mixed[n]
                ta_copy(target).start()

            @pl.when(target == frame)
            def _():
                att_time[me, frame] = mixed[n]
                forward(frame)

        return carry

    lax.fori_loop(0, STEPS, time_attention, 0)
    swap_weights(2)

    def relay(origin):
        ta_arrival(origin).wait_recv()
        forward(origin)

    others(relay)
    load_out(1).wait()
    finish_weights(2)

    def result_copy(index):
        span = chunk_rows(index)
        return pltpu.make_async_copy(stream.at[span], result_ref.at[0, span], out_sem.at[index])

    def time_project(i, carry):
        index = lax.rem(frame // per_chunk + chunks - i, chunks)
        span = chunk_rows(index)
        for n in range(per_chunk):
            for distance in range(1, parts):
                att_time_copy(index * per_chunk + n, distance).wait_recv()
        summed = jnp.zeros((chunk, part_width), jnp.float32)
        for part in range(parts):
            attended = att_time[part, pl.ds(index * per_chunk, per_chunk)].astype(jnp.float32)
            summed = summed + jnp.dot(
                attended.reshape(chunk, heads_width).astype(jnp.bfloat16), out_weight(1, part),
                preferred_element_type=jnp.float32,
            ).astype(jnp.bfloat16).astype(jnp.float32)
        stream[span, :] = stream[span, :] + mods[1, 2:3] * summed
        result_copy(index).start()
        return carry

    lax.fori_loop(0, chunks, time_project, 0)

    def drain(i, carry):
        kv_copy(i).wait_send()
        for distance in range(1, parts):
            h_copy(i, distance).wait_send()
        result_copy(i).wait()
        return carry

    lax.fori_loop(0, chunks, drain, 0)

    def drain_steps(i, carry):
        for distance in range(1, parts):
            part_copy(i, distance).wait_send()
        return carry

    lax.fori_loop(0, STEPS, drain_steps, 0)

    def drain_blocks(i, carry):
        for distance in range(1, parts):
            att_space_copy(i, distance).wait_send()
        return carry

    lax.fori_loop(0, query_blocks, drain_blocks, 0)

    def drain_pieces(i, carry):
        for distance in range(1, parts):
            att_time_copy(i, distance).wait_send()
        return carry

    lax.fori_loop(0, frames, drain_pieces, 0)

    def drain_other(target):
        tq_copy(target).wait_send()
        ta_copy(target).wait_send()

    others(drain_other)
    for distance in range(1, parts):
        for layer in range(2):
            stat_copy(layer, distance).wait_send()
        for kind in range(3):
            weight_copy(kind, distance).wait_send()
            core_copy(kind, distance).wait_send()
            for step in range(half_ring):
                twin_copy(kind, distance, step, place).wait_send()
                if step:
                    ring_copy(kind, distance, step, place).wait_send()


def on_device(tokens, block_mask, space_qkv, space_out, space_mod, time_qkv, time_out, time_mod):
    videos, rows, part_width = tokens.shape
    heads_width = space_qkv.shape[2]
    frames = lax.axis_size("seq") // 2
    parts = lax.axis_size("fsdp")
    piece = rows // frames
    chunk = rows // STEPS
    chunks = rows // chunk
    blocks = rows // BLOCK
    width = part_width * parts
    bf16, f32 = jnp.bfloat16, jnp.float32
    dma = pltpu.SemaphoreType.DMA
    cut_rows = lambda weight: weight.reshape(RING, 2, heads_width // (2 * RING), width)
    hbm = pl.BlockSpec(memory_space=pl.ANY)
    scratch = [
        pltpu.VMEM((rows, part_width), f32),
        pltpu.VMEM((rows, 128), f32),
        pltpu.VMEM((rows, 3 * heads_width), f32),
        pltpu.VMEM((rows, heads_width), bf16),
        pltpu.VMEM((2, 2, rows, heads_width), bf16),
        pltpu.VMEM((frames, piece, 3 * heads_width), bf16),
        pltpu.VMEM((frames, piece, 3 * heads_width), bf16),
        pltpu.VMEM((frames, piece, heads_width), bf16),
        pltpu.VMEM((width, 3 * heads_width), bf16),
        pltpu.VMEM((parts, 3, part_width, heads_width), bf16),
        pltpu.VMEM((2, parts, RING, 2, heads_width // (2 * RING), part_width), bf16),
        pltpu.VMEM((2, 3, part_width), f32),
        pltpu.VMEM((2, parts, 8, rows), f32),
        pltpu.VMEM((parts, rows, part_width), bf16),
        pltpu.VMEM((rows, part_width), bf16),
        pltpu.VMEM((parts, rows, 3 * heads_width), bf16),
        pltpu.VMEM((parts, rows, 3 * heads_width), bf16),
        pltpu.VMEM((parts, rows, heads_width), bf16),
        pltpu.VMEM((parts, frames, piece, heads_width), bf16),
        dma, dma((3,)), dma, dma((2,)), dma((2,)), dma((chunks,)),
        dma((2, parts)), dma((2, parts)),
        dma((parts, chunks)), dma((parts, chunks)),
        dma((parts, STEPS)), dma((parts, STEPS)),
        dma((chunks,)), dma((chunks,)),
        dma((parts, blocks)), dma((parts, blocks)),
        dma((parts, frames)), dma((parts, frames)),
        dma((3, parts)), dma((3, parts)),
        dma((3, parts, RING)), dma((3, parts, RING)),
        dma((3, parts)), dma((3, parts)),
        dma((frames,)), dma((frames,)),
        dma((frames,)), dma((frames,)),
    ]
    sizes = (frames, parts, rows, part_width, heads_width, chunk)
    return pl.pallas_call(
        functools.partial(sublayers, sizes),
        out_shape=jax.ShapeDtypeStruct(tokens.shape, f32),
        in_specs=[pl.BlockSpec(memory_space=pltpu.SMEM)] + [hbm] * 7,
        out_specs=pl.BlockSpec(memory_space=pltpu.VMEM),
        scratch_shapes=scratch,
        compiler_params=pltpu.CompilerParams(
            collective_id=0, has_side_effects=True, vmem_limit_bytes=58 * 1024 * 1024
        ),
        cost_estimate=pl.CostEstimate(
            flops=4 * rows * width * 4 * heads_width, bytes_accessed=20 * 1024 * 1024,
            transcendentals=1024 * 1024,
        ),
    )(
        jnp.swapaxes(block_mask, 0, 1), tokens, jnp.swapaxes(space_qkv, 0, 1), cut_rows(space_out), space_mod,
        jnp.swapaxes(time_qkv, 0, 1), cut_rows(time_out), time_mod,
    )


def solution(mesh):
    placed = (
        P(None, "seq", "fsdp"),
        P(),
        P(None, None, "fsdp"),
        P("fsdp", None),
        P(),
        P(None, None, "fsdp"),
        P("fsdp", None),
        P(),
    )
    return jax.shard_map(
        on_device, mesh=mesh, in_specs=placed, out_specs=P(None, "seq", "fsdp"), check_vma=False
    )
```
